256 devices in a mesh: ctx: 64 (over z, y, core), tp: 4 (over x).
Axes of the slice: x: 4, y: 4, z: 8, core: 2. Of those that a mesh axis runs over, the one named last changes fastest.
Arguments:
- queries: bfloat16 [16384, 64, 128], P('ctx', 'tp'), may hold values from -4 to 4
- keys: bfloat16 [16384, 8, 128], P('ctx', 'tp'), may hold values from -4 to 4
- values: bfloat16 [16384, 8, 128], P('ctx', 'tp'), may hold values from -6 to 6
- attn_out: bfloat16 [16384, 64, 128], P('ctx', 'tp'), may hold values from -6 to 6
- grad_out: bfloat16 [16384, 64, 128], P('ctx', 'tp'), may hold values from -4 to 4
- log_norm: float32 [64, 16384], P('tp', 'ctx'), may hold values from 2 to 4
- doc_lengths: int32 [32], replicated, may hold values from 1 to 1024, 16384 in all
- doc_weight: int32 [32], replicated, may hold values from 4 to 22
Outputs:
- grad_queries: float32 [16384, 64, 128], P('ctx', 'tp')
- grad_keys: float32 [16384, 8, 128], P('ctx', 'tp')
- grad_values: float32 [16384, 8, 128], P('ctx', 'tp')
The draws below stay inside these ranges and needn't reach their ends.
Inputs may be any that keep to these rules, and one draw needn't show every extreme that they name: doc_lengths sum to 16384; the longest document has exactly 1024 tokens.
All inputs are finite; a program needn't handle non-finite values.
Results may differ from the reference program's by a relative error of at most 0.0041.
Values may be sent and summed in bfloat16 or wider, within the bound.
A program may use at most 128 MiB of HBM per device.

```python
import math
import jax
import jax.numpy as jnp
import numpy as np
from jax import lax

HD = 128
GROUP = 8
TOK_DEV = 256
SPAN = 4
KVHEADS = 8
HEADS = 64
TOKENS = 16384
DOCS = 32
DOC_MOST = 1024


def draw_doc_weight(key, part):
    key = jax.random.fold_in(key, 11)
    doc_number = jnp.arange(DOCS, dtype=jnp.int32)
    rising = 4 + 16 * doc_number // DOCS
    jitter = jax.random.randint(key, (DOCS,), 0, 4, dtype=jnp.int32)
    jitter = jnp.where(doc_number == 0, 0, jnp.where(doc_number == DOCS - 1, 3, jitter))
    return (rising + jitter).astype(jnp.int32)


def steps_of(stream_key, dims, cuts, low, top_value):
    factor_of = 1.0
    for dim, parts in cuts:
        steps = jax.random.uniform(jax.random.fold_in(jax.random.fold_in(stream_key, 6), dim), (parts,), jnp.float32, low / len(cuts), top_value / len(cuts))
        factor_of = factor_of * jnp.repeat(jnp.exp(steps), dims[dim] // parts).reshape((-1,) + (1,) * (len(dims) - 1 - dim))
    return factor_of


def profile(count, total, limit, skew):
    loads = [(1 << 20) // math.isqrt(standing ** skew) + 1 for standing in range(2, count + 1)]
    surplus, given = total - limit - (count - 1), [1] * (count - 1)
    while surplus > 0:
        movable = [i for i in range(count - 1) if given[i] < limit]
        mass, remaining = sum([loads[i] for i in movable]), surplus
        for i in movable:
            extra = min(limit - given[i], max(1, remaining * loads[i] // mass), surplus)
            given[i] = given[i] + extra
            surplus = surplus - extra
    return np.array([limit] + given)


def uneven(stream_key, number_of, total, bound, skew):
    if number_of == 2:
        one = jax.random.randint(stream_key, (), max(1, total - bound), min(bound, total - 1) + 1)
        return jnp.stack([one, total - one])
    sizes = jnp.asarray(profile(number_of, total, bound, skew), jnp.int32)
    couples = (number_of - 1) // 2
    donor, receiver = sizes[1:1 + 2 * couples:2], sizes[2:2 + 2 * couples:2]
    margin = jnp.minimum(donor - 1, bound - receiver)
    passed = jax.random.randint(jax.random.fold_in(stream_key, 1), (couples,), 0, 1 << 20) % (margin + 1)
    sizes = sizes.at[1:1 + 2 * couples:2].set(donor - passed).at[2:2 + 2 * couples:2].set(receiver + passed)
    return sizes[jax.random.permutation(jax.random.fold_in(stream_key, 2), number_of)]


def scatter_about(rng, extent, scale, limit, cuts=(), kind=jnp.bfloat16):
    array = jax.random.normal(rng, extent, jnp.float32) * scale
    if len(cuts) > 0:
        array = steps_of(rng, extent, cuts, -0.22, 0.18) * array
    return jnp.clip(array, min=-limit, max=limit).astype(kind)


def setup_inputs(seed: int = 0) -> dict:
    seeds = jax.random.split(jax.random.key(seed), 9)
    return {
        "queries": scatter_about(seeds[0], (TOKENS, HEADS, HD), 1.0, 4.0, ((0, 64), (1, 4))),
        "keys": scatter_about(seeds[1], (TOKENS, KVHEADS, HD), 1.0, 4.0, ((0, 64), (1, 4))),
        "values": scatter_about(seeds[2], (TOKENS, KVHEADS, HD), 1.0, 6.0, ((0, 64), (1, 4))),
        "attn_out": scatter_about(seeds[3], (TOKENS, HEADS, HD), 1.0, 6.0, ((0, 64), (1, 4))),
        "grad_out": scatter_about(seeds[4], (TOKENS, HEADS, HD), 0.3, 4.0, ((0, 64), (1, 4))),
        "log_norm": jnp.clip(2.0 + 2.0 * jax.random.uniform(seeds[5], (HEADS, TOKENS), jnp.float32) ** steps_of(seeds[5], (HEADS, TOKENS), ((0, 4), (1, 64)), -0.2, 0.2), 2.0, 4.0),
        "doc_lengths": uneven(seeds[6], DOCS, TOKENS, DOC_MOST, 2).astype(jnp.int32),
        "doc_weight": draw_doc_weight(jax.random.fold_in(seeds[8], 71), 0),
    }


def doc_index(positions, doc_ends):
    counts = jnp.sum((positions[:, None] >= doc_ends[None, :]).astype(jnp.int32), axis=1)
    return jnp.where(positions >= 0, counts, -1).astype(jnp.int32)


def reference(queries, keys, values, attn_out, grad_out, log_norm, doc_lengths, doc_weight):
    doc_ends = jnp.cumsum(doc_lengths).astype(jnp.int32)
    positions = jnp.arange(TOKENS, dtype=jnp.int32)
    token_docs = doc_index(positions, doc_ends)
    token_weight = doc_weight[token_docs].astype(jnp.float32)
    weight_total = jnp.sum(token_weight)
    token_scale = token_weight * TOKENS / weight_total
    row_delta = token_scale[:, None] * jnp.sum(grad_out.astype(jnp.float32) * attn_out.astype(jnp.float32), axis=-1)
    scaled_grad = (grad_out.astype(jnp.float32) * token_scale[:, None, None]).astype(jnp.bfloat16)
    key_reach = SPAN * TOK_DEV
    key_window = key_reach + TOK_DEV
    padded_keys = jnp.concatenate([jnp.zeros((key_reach, KVHEADS, HD), jnp.bfloat16), keys], axis=0)
    padded_values = jnp.concatenate([jnp.zeros((key_reach, KVHEADS, HD), jnp.bfloat16), values], axis=0)
    key_docs = doc_index(jnp.arange(TOKENS + key_reach, dtype=jnp.int32) - key_reach, doc_ends)
    score_scale = HD ** -0.5

    def block_step(running, block_index):
        grad_k, grad_v = running
        row_start = (block_index * TOK_DEV).astype(jnp.int32)
        q_blk = lax.dynamic_slice_in_dim(queries, row_start, TOK_DEV, 0).astype(jnp.float32).reshape(TOK_DEV, KVHEADS, GROUP, HD)
        g_blk = lax.dynamic_slice_in_dim(scaled_grad, row_start, TOK_DEV, 0).astype(jnp.float32).reshape(TOK_DEV, KVHEADS, GROUP, HD)
        norm_blk = lax.dynamic_slice_in_dim(log_norm, row_start, TOK_DEV, 1).reshape(KVHEADS, GROUP, TOK_DEV)
        delta_blk = lax.dynamic_slice_in_dim(row_delta, row_start, TOK_DEV, 0).T.reshape(KVHEADS, GROUP, TOK_DEV)
        k_win = lax.dynamic_slice_in_dim(padded_keys, row_start, key_window, 0).astype(jnp.float32)
        v_win = lax.dynamic_slice_in_dim(padded_values, row_start, key_window, 0).astype(jnp.float32)
        q_docs = lax.dynamic_slice_in_dim(token_docs, row_start, TOK_DEV, 0)
        k_docs = lax.dynamic_slice_in_dim(key_docs, row_start, key_window, 0)
        q_pos = row_start + jnp.arange(TOK_DEV, dtype=jnp.int32)
        k_pos = row_start - key_reach + jnp.arange(key_window, dtype=jnp.int32)
        allowed = (q_docs[:, None] == k_docs[None, :]) & (k_pos[None, :] <= q_pos[:, None])
        scores = jnp.einsum('ihgd,jhd->hgij', q_blk, k_win) * score_scale
        prob_full = jnp.where(allowed, jnp.exp(scores - norm_blk[..., None]), 0.0)
        prob_low = lax.optimization_barrier(prob_full.astype(jnp.bfloat16)).astype(jnp.float32)
        grad_v_win = jnp.einsum('hgij,ihgd->jhd', prob_low, g_blk)
        grad_prob = jnp.einsum('ihgd,jhd->hgij', g_blk, v_win)
        grad_score = lax.optimization_barrier((prob_full * (grad_prob - delta_blk[..., None])).astype(jnp.bfloat16)).astype(jnp.float32)
        grad_q = jnp.einsum('hgij,jhd->ihgd', grad_score, k_win) * score_scale
        grad_k_win = jnp.einsum('hgij,ihgd->jhd', grad_score, q_blk) * score_scale
        grad_k = lax.dynamic_update_slice_in_dim(grad_k, lax.dynamic_slice_in_dim(grad_k, row_start, key_window, 0) + grad_k_win, row_start, 0)
        grad_v = lax.dynamic_update_slice_in_dim(grad_v, lax.dynamic_slice_in_dim(grad_v, row_start, key_window, 0) + grad_v_win, row_start, 0)
        return (grad_k, grad_v), grad_q.reshape(TOK_DEV, HEADS, HD)

    empty = jnp.zeros((TOKENS + key_reach, KVHEADS, HD), jnp.float32)
    (grad_k, grad_v), grad_q = lax.scan(block_step, (empty, empty), jnp.arange(TOKENS // TOK_DEV, dtype=jnp.int32))
    return grad_q.reshape(TOKENS, HEADS, HD), grad_k[key_reach:], grad_v[key_reach:]
```

```python
import functools

import jax
import jax.numpy as jnp
from jax import lax
from jax.experimental import pallas as pl
from jax.experimental.pallas import tpu as pltpu
from jax.sharding import PartitionSpec as P

MESH = pl.DeviceIdType.MESH
F32, BF16 = jnp.float32, jnp.bfloat16
NT = (((1,), (1,)), ((), ()))
NN = (((1,), (0,)), ((), ()))

TOK = 256
HD = 128
GROUP = 8
DOCS = 32
SCALE = HD ** -0.5
DOC_LANE = 64
FAR_AWAY = 16384.0


def dot(a, b, dims):
    return lax.dot_general(a, b, dims, preferred_element_type=F32)


def iota(shape, dim):
    return lax.broadcasted_iota(jnp.int32, shape, dim)


def kernel(n_ctx, q_hbm, k_hbm, v_hbm, o_hbm, g_hbm, ln_hbm, dl_ref, dw_ref, dq_ref, dk_ref, dv_ref,
           q_in, k_in, v_in, o_in, g_in, ln_in,
           kv_send, kvs, kaug, q_all, g_all, a_all, q_s, g_s, a_s, xaug, yaug, qt, gt, go_hi, go_lo,
           p_buf, d_buf, own_part, mate_part, ret_send, ret_recv, dq_send, dq_hm, totals,
           in_sem, kv_ssem, kv_rsem, x_ssem, x_rsem, r_ssem, r_rsem, m_ssem, m_rsem, dq_ssem, dq_rsem):
    me = lax.axis_index("ctx")
    tp = lax.axis_index("tp")
    core = lax.rem(me, 2)
    chip2 = me - core
    mate = chip2 + 1 - core

    def at(chips, j):
        return (lax.rem(chip2 + 2 * chips + j + n_ctx, n_ctx), tp)

    def remote(src, dst, ssem, rsem, dev):
        return pltpu.make_async_remote_copy(src_ref=src, dst_ref=dst, send_sem=ssem, recv_sem=rsem,
                                            device_id=dev, device_id_type=MESH)

    mate_dev = (mate, tp)
    loads = [pltpu.make_async_copy(s, d, in_sem.at[i]) for i, (s, d) in enumerate(
        [(k_hbm, k_in), (v_hbm, v_in), (g_hbm, g_in), (o_hbm, o_in), (q_hbm, q_in), (ln_hbm, ln_in)])]
    for load in loads:
        load.start()
    barrier = pltpu.get_barrier_semaphore()
    peers = [mate_dev] + [at(d, j) for d in (1, -1, 2, -2) for j in (0, 1)]
    for peer in peers:
        pl.semaphore_signal(barrier, inc=1, device_id=peer, device_id_type=MESH)

    loads[0].wait()
    kv_send[:, 0] = jnp.swapaxes(k_in[...], 0, 1)
    loads[1].wait()
    kv_send[:, 1] = jnp.swapaxes(v_in[...], 0, 1)
    kvs[4 + core] = kv_send[core]
    pl.semaphore_wait(barrier, len(peers))

    sends = [remote(kv_send.at[1 - core], kvs.at[4 + core], kv_ssem.at[0], kv_rsem.at[4 + core], mate_dev)]
    for i, (chips, slot) in enumerate(((1, 2), (2, 0))):
        for h in (0, 1):
            sends.append(remote(kv_send.at[h], kvs.at[slot + core], kv_ssem.at[1 + 2 * i + h],
                                kv_rsem.at[slot + core], at(chips, h)))
    for s in sends:
        s.start()

    def wait_block(kb):
        remote(kv_send.at[0], kvs.at[kb], kv_ssem.at[0], kv_rsem.at[kb], mate_dev).wait_recv()

    def wait_return(i):
        remote(ret_send.at[0, 0], ret_recv.at[i], r_ssem.at[0], r_rsem.at[i], mate_dev).wait_recv()

    lane1 = iota((1, HD), 1)
    starts = jnp.full((1, HD), 1 << 30, jnp.int32)
    ends = jnp.zeros((1, HD), jnp.int32)
    weights = jnp.zeros((1, HD), F32)
    run = jnp.int32(0)
    total = jnp.int32(0)
    for d in range(DOCS):
        here = lane1 == DOC_LANE + d
        length = dl_ref[d]
        weight = dw_ref[d]
        starts = jnp.where(here, run, starts)
        run = run + length
        ends = jnp.where(here, run, ends)
        weights = jnp.where(here, weight.astype(F32), weights)
        total = total + length * weight

    rows = iota((TOK, HD), 0)
    lanes = iota((TOK, HD), 1)

    def one_hot(block):
        pos = block * TOK + rows
        return (pos >= starts) & (pos < ends)

    for kb in range(6):
        hot = one_hot(chip2 - 4 + kb)
        extra = jnp.where(lanes < 48, 1.0, jnp.where((lanes >= DOC_LANE) & (lanes < DOC_LANE + DOCS) & ~hot, -FAR_AWAY, 0.0))
        kaug[kb] = extra.astype(BF16)

    scale = jnp.sum(jnp.where(one_hot(me), weights, 0.0), axis=1, keepdims=True)
    scale = scale * float(n_ctx * TOK) / total.astype(F32)
    scale = jnp.broadcast_to(scale, (TOK, HD))

    loads[2].wait()
    g_all[...] = jnp.swapaxes(g_in[...], 0, 1)
    loads[3].wait()
    q_all[...] = jnp.swapaxes(o_in[...], 0, 1)
    for h in range(2 * GROUP):
        g = g_all[h].astype(F32)
        go = g * q_all[h].astype(F32)
        hi = go.astype(BF16)
        cols = pl.ds(h * HD, HD)
        go_hi[:, cols] = hi
        go_lo[:, cols] = (go - hi.astype(F32)).astype(BF16)
        g_all[h] = (g * scale).astype(BF16)
    send_g = remote(g_all.at[pl.ds(GROUP * (1 - core), GROUP)], g_s.at[core], x_ssem.at[0], x_rsem.at[0], mate_dev)
    send_g.start()
    loads[4].wait()
    q_all[...] = jnp.swapaxes(q_in[...], 0, 1)
    send_q = remote(q_all.at[pl.ds(GROUP * (1 - core), GROUP)], q_s.at[core], x_ssem.at[1], x_rsem.at[1], mate_dev)
    send_q.start()
    g_s[core] = g_all[pl.ds(GROUP * core, GROUP)]
    q_s[core] = q_all[pl.ds(GROUP * core, GROUP)]

    big = iota((2 * GROUP * HD, HD), 0) // HD
    bl = iota((2 * GROUP * HD, HD), 1)
    pick = jnp.where((bl >= DOC_LANE) & (bl < DOC_LANE + 48) & (lax.rem(bl, 16) == big), 1.0, 0.0).astype(BF16)
    delta = dot(go_hi[...], pick, NN) + dot(go_lo[...], pick, NN)
    loads[5].wait()
    ln = ln_in[...]
    norm = jnp.concatenate([ln, ln, ln, jnp.zeros((80, TOK), F32)], axis=0).T
    z = jnp.where(lanes < 48, norm * (-(HD ** 0.5)), -(delta * scale))
    hi = z.astype(BF16)
    rest = z - hi.astype(F32)
    mid = rest.astype(BF16)
    low = (rest - mid.astype(F32)).astype(BF16)
    term = lax.rem(lanes, 64) // 16
    a_all[...] = jnp.where(term == 0, hi.astype(F32), jnp.where(term == 1, mid.astype(F32), low.astype(F32))).astype(BF16)
    send_a = remote(a_all, a_s.at[core], x_ssem.at[2], x_rsem.at[2], mate_dev)
    send_a.start()
    a_s[core] = a_all[...]

    def prepare(qb):
        a = a_s[qb].astype(F32)
        hot = one_hot(chip2 + qb)
        base = jnp.where(hot, 1.0, 0.0)
        slot = lax.rem(lanes, 16)
        for g in range(GROUP):
            mine = slot == GROUP * core + g
            xaug[qb, g] = jnp.where(mine & (lanes < 48), a, base).astype(BF16)
            yaug[qb, g] = jnp.where(mine & (lanes >= 64) & (lanes < 112), a, 0.0).astype(BF16)
            cols = pl.ds(pl.multiple_of((qb * GROUP + g) * TOK, TOK), TOK)
            qt[:, cols] = q_s[qb, g].T
            gt[:, cols] = g_s[qb, g].T

    ones = jnp.ones((TOK, HD), BF16)

    def keys_of(kbs):
        return jnp.concatenate([jnp.concatenate([kvs[kb, 0], kaug[kb]], axis=1) for kb in kbs], axis=0)

    def values_of(kbs):
        return jnp.concatenate([jnp.concatenate([kvs[kb, 1], ones], axis=1) for kb in kbs], axis=0)

    causal = iota((TOK, TOK), 0) >= iota((TOK, TOK), 1)

    def scores(qb, kbs, diagonal=False):
        width = TOK * len(kbs)
        cols = pl.ds(kbs[0] * TOK, width)
        keys, values = keys_of(kbs), values_of(kbs)
        for g in range(GROUP):
            x = jnp.concatenate([q_s[qb, g], xaug[qb, g]], axis=1)
            y = jnp.concatenate([g_s[qb, g], yaug[qb, g]], axis=1)
            p = jnp.exp(dot(x, keys, NT) * SCALE)
            if diagonal:
                keep = causal if len(kbs) == 1 else jnp.concatenate([jnp.ones((TOK, TOK), jnp.bool_), causal], axis=1)
                p = jnp.where(keep, p, 0.0)
            ds = p * dot(y, values, NT)
            at_rows = pl.ds((qb * GROUP + g) * TOK, TOK)
            p_buf[at_rows, cols] = p.astype(BF16)
            d_buf[at_rows, cols] = ds.astype(BF16)

    half = GROUP * TOK

    def kv_grads(first_row, kb, count):
        r = pl.ds(first_row, 2 * half - first_row) if first_row else slice(None)
        c = pl.ds(kb * TOK, count * TOK)
        return dot(qt[:, r], d_buf[r, c], NN), dot(gt[:, r], p_buf[r, c], NN)

    prepare(core)
    wait_block(5 - core)
    for s in (send_g, send_q, send_a):
        s.wait_recv()
    prepare(1 - core)

    scores(0, (4,), True)
    scores(1, (4, 5), True)
    dk0, dv0 = kv_grads(0, 4, 1)
    dk1, dv1 = kv_grads(half, 5, 1)
    own_part[0, 0] = dk0
    own_part[0, 1] = dv0
    own_part[1, 0] = dk1
    own_part[1, 1] = dv1
    send_m = remote(own_part.at[1 - core], mate_part, m_ssem.at[0], m_rsem.at[0], mate_dev)
    send_m.start()

    def give_back(stage, slot, chips):
        out = []
        for j in (0, 1):
            c = remote(ret_send.at[stage, j], ret_recv.at[slot + core], r_ssem.at[2 * stage + j], r_rsem.at[slot + core],
                       at(chips, j))
            c.start()
            out.append(c)
        return out

    wait_block(2)
    wait_block(3)
    scores(0, (2, 3))
    scores(1, (2, 3))
    dk, dv = kv_grads(0, 2, 2)
    for j in (0, 1):
        ret_send[0, j, 0] = dk[:, j * TOK:(j + 1) * TOK].astype(BF16)
        ret_send[0, j, 1] = dv[:, j * TOK:(j + 1) * TOK].astype(BF16)
    returns = give_back(0, 0, -1)

    wait_block(0)
    wait_block(1)
    scores(0, (0, 1))
    scores(1, (1,))
    r0 = pl.ds(0, half)
    c0 = pl.ds(0, TOK)
    ret_send[1, 0, 0] = dot(qt[:, r0], d_buf[r0, c0], NN).astype(BF16)
    ret_send[1, 0, 1] = dot(gt[:, r0], p_buf[r0, c0], NN).astype(BF16)
    dk, dv = kv_grads(0, 1, 1)
    ret_send[1, 1, 0] = dk.astype(BF16)
    ret_send[1, 1, 1] = dv.astype(BF16)
    returns += give_back(1, 2, -2)

    def query_grads(qb, out_at):
        keys = kvs[pl.ds(qb, 5), 0].reshape(5 * TOK, HD)
        for g in range(GROUP):
            r = pl.ds(pl.multiple_of((qb * GROUP + g) * TOK, TOK), TOK)
            c = pl.ds(pl.multiple_of(qb * TOK, TOK), 5 * TOK)
            out_at(g, dot(d_buf[r, c], keys, NN) * SCALE)

    def to_mate(g, x):
        dq_send[g] = x

    def to_own(g, x):
        dq_hm[GROUP * core + g] = x

    query_grads(1 - core, to_mate)
    send_dq = remote(dq_send, dq_hm.at[pl.ds(GROUP * core, GROUP)], dq_ssem.at[0], dq_rsem.at[0], mate_dev)
    send_dq.start()
    query_grads(core, to_own)
    send_dq.wait_recv()
    dq_ref[...] = jnp.swapaxes(dq_hm[...], 0, 1)

    send_m.wait_recv()
    for i in range(4):
        wait_return(i)

    def add_up(part, h):
        x = part + ret_recv[h].astype(F32) + ret_recv[2 + h].astype(F32)
        totals[h, 0] = x[0].T * SCALE
        totals[h, 1] = x[1].T

    add_up(own_part[core], core)
    add_up(mate_part[...], 1 - core)
    dk_ref[...] = jnp.swapaxes(totals[:, 0], 0, 1)
    dv_ref[...] = jnp.swapaxes(totals[:, 1], 0, 1)
    for s in sends + [send_g, send_q, send_a, send_m, send_dq] + returns:
        s.wait_send()


def shards(n_ctx, queries, keys, values, attn_out, grad_out, log_norm, doc_lengths, doc_weight):
    any_space = pl.BlockSpec(memory_space=pl.ANY)
    smem = pl.BlockSpec(memory_space=pltpu.SMEM)
    vmem = pl.BlockSpec(memory_space=pltpu.VMEM)
    dma = pltpu.SemaphoreType.DMA
    q_shape, k_shape = queries.shape, keys.shape
    wide = 2 * GROUP * TOK

    def buf(*shape, dtype=BF16):
        return pltpu.VMEM(shape, dtype)

    return pl.pallas_call(
        functools.partial(kernel, n_ctx),
        out_shape=(
            jax.ShapeDtypeStruct(q_shape, F32),
            jax.ShapeDtypeStruct(k_shape, F32),
            jax.ShapeDtypeStruct(k_shape, F32),
        ),
        in_specs=[any_space] * 6 + [smem] * 2,
        out_specs=(vmem, vmem, vmem),
        scratch_shapes=[
            buf(*q_shape), buf(*k_shape), buf(*k_shape), buf(*q_shape), buf(*q_shape), buf(2 * GROUP, TOK, dtype=F32),
            buf(2, 2, TOK, HD), buf(6, 2, TOK, HD), buf(6, TOK, HD),
            buf(2 * GROUP, TOK, HD), buf(2 * GROUP, TOK, HD), buf(TOK, HD),
            buf(2, GROUP, TOK, HD), buf(2, GROUP, TOK, HD), buf(2, TOK, HD),
            buf(2, GROUP, TOK, HD), buf(2, GROUP, TOK, HD),
            buf(HD, wide), buf(HD, wide), buf(TOK, 2 * GROUP * HD), buf(TOK, 2 * GROUP * HD),
            buf(wide, 6 * TOK), buf(wide, 6 * TOK),
            buf(2, 2, HD, TOK, dtype=F32), buf(2, HD, TOK, dtype=F32),
            buf(2, 2, 2, HD, TOK), buf(4, 2, HD, TOK),
            buf(GROUP, TOK, HD, dtype=F32), buf(2 * GROUP, TOK, HD, dtype=F32), buf(2, 2, TOK, HD, dtype=F32),
            dma((6,)), dma((5,)), dma((6,)), dma((3,)), dma((3,)), dma((4,)), dma((4,)), dma((1,)), dma((1,)),
            dma((1,)), dma((1,)),
        ],
        compiler_params=pltpu.CompilerParams(collective_id=0, has_side_effects=True, vmem_limit_bytes=60 << 20),
    )(queries, keys, values, attn_out, grad_out, log_norm, doc_lengths, doc_weight)


def solution(mesh):
    return jax.shard_map(
        functools.partial(shards, mesh.shape["ctx"]),
        mesh=mesh,
        in_specs=(
            P("ctx", "tp", None),
            P("ctx", "tp", None),
            P("ctx", "tp", None),
            P("ctx", "tp", None),
            P("ctx", "tp", None),
            P("tp", "ctx"),
            P(),
            P(),
        ),
        out_specs=(P("ctx", "tp", None), P("ctx", "tp", None), P("ctx", "tp", None)),
        check_vma=False,
    )
```

```python
import functools

import jax
import jax.numpy as jnp
from jax import lax
from jax.experimental import pallas as pl
from jax.experimental.pallas import tpu as pltpu
from jax.sharding import PartitionSpec as P

MESH = pl.DeviceIdType.MESH
F32, BF16 = jnp.float32, jnp.bfloat16
NT = (((1,), (1,)), ((), ()))
NN = (((1,), (0,)), ((), ()))

TOK = 256
HD = 128
GROUP = 8
DOCS = 32
SCALE = HD ** -0.5
DOC_LANE = 64
FAR_AWAY = 16384.0


def dot(a, b, dims):
    return lax.dot_general(a, b, dims, preferred_element_type=F32)


def iota(shape, dim):
    return lax.broadcasted_iota(jnp.int32, shape, dim)


def kernel(n_ctx, q_hbm, k_hbm, v_hbm, o_hbm, g_hbm, ln_hbm, dl_ref, dw_ref, dq_ref, dk_ref, dv_ref,
           q_in, k_in, v_in, o_in, g_in, ln_in,
           kv_send, kvs, kaug, q_all, g_all, a_all, q_s, g_s, a_s, xaug, yaug, qt, gt, go_hi, go_lo,
           p_buf, d_buf, own_part, mate_part, ret_send, ret_recv, dq_acc, dq_mate, totals,
           in_sem, kv_ssem, kv_rsem, x_ssem, x_rsem, r_ssem, r_rsem, m_ssem, m_rsem, dq_ssem, dq_rsem):
    me = lax.axis_index("ctx")
    tp = lax.axis_index("tp")
    core = lax.rem(me, 2)
    chip2 = me - core
    mate = chip2 + 1 - core

    def at(chips, j):
        return (lax.rem(chip2 + 2 * chips + j + n_ctx, n_ctx), tp)

    def remote(src, dst, ssem, rsem, dev):
        return pltpu.make_async_remote_copy(src_ref=src, dst_ref=dst, send_sem=ssem, recv_sem=rsem,
                                            device_id=dev, device_id_type=MESH)

    mate_dev = (mate, tp)
    loads = [pltpu.make_async_copy(s, d, in_sem.at[i]) for i, (s, d) in enumerate(
        [(k_hbm, k_in), (v_hbm, v_in), (g_hbm, g_in), (o_hbm, o_in), (q_hbm, q_in), (ln_hbm, ln_in)])]
    for load in loads:
        load.start()
    barrier = pltpu.get_barrier_semaphore()
    peers = [mate_dev] + [at(d, j) for d in (1, -1, 2, -2) for j in (0, 1)]
    for peer in peers:
        pl.semaphore_signal(barrier, inc=1, device_id=peer, device_id_type=MESH)

    loads[0].wait()
    kv_send[:, 0] = jnp.swapaxes(k_in[...], 0, 1)
    loads[1].wait()
    kv_send[:, 1] = jnp.swapaxes(v_in[...], 0, 1)
    kvs[4 + core] = kv_send[core]
    pl.semaphore_wait(barrier, len(peers))

    sends = [remote(kv_send.at[1 - core], kvs.at[4 + core], kv_ssem.at[0], kv_rsem.at[4 + core], mate_dev)]
    for h in (0, 1):
        sends.append(remote(kv_send.at[h], kvs.at[2 + core], kv_ssem.at[1 + h], kv_rsem.at[2 + core], at(1, h)))
    for s in sends:
        s.start()

    def wait_block(kb):
        remote(kv_send.at[0], kvs.at[kb], kv_ssem.at[0], kv_rsem.at[kb], mate_dev).wait_recv()

    def wait_return(i):
        remote(ret_send.at[0], ret_recv.at[i], r_ssem.at[0], r_rsem.at[i], mate_dev).wait_recv()

    lane1 = iota((1, HD), 1)
    starts = jnp.full((1, HD), 1 << 30, jnp.int32)
    ends = jnp.zeros((1, HD), jnp.int32)
    weights = jnp.zeros((1, HD), F32)
    run = jnp.int32(0)
    total = jnp.int32(0)
    for d in range(DOCS):
        here = lane1 == DOC_LANE + d
        length = dl_ref[d]
        weight = dw_ref[d]
        starts = jnp.where(here, run, starts)
        run = run + length
        ends = jnp.where(here, run, ends)
        weights = jnp.where(here, weight.astype(F32), weights)
        total = total + length * weight

    rows = iota((TOK, HD), 0)
    lanes = iota((TOK, HD), 1)

    def one_hot(block):
        pos = block * TOK + rows
        return (pos >= starts) & (pos < ends)

    for kb in range(6):
        hot = one_hot(chip2 - 4 + kb)
        extra = jnp.where(lanes < 48, 1.0, jnp.where((lanes >= DOC_LANE) & (lanes < DOC_LANE + DOCS) & ~hot, -FAR_AWAY, 0.0))
        kaug[kb] = extra.astype(BF16)

    scale = jnp.sum(jnp.where(one_hot(me), weights, 0.0), axis=1, keepdims=True)
    scale = scale * float(n_ctx * TOK) / total.astype(F32)
    scale = jnp.broadcast_to(scale, (TOK, HD))

    loads[2].wait()
    g_all[...] = jnp.swapaxes(g_in[...], 0, 1)
    loads[3].wait()
    q_all[...] = jnp.swapaxes(o_in[...], 0, 1)
    for h in range(2 * GROUP):
        g = g_all[h].astype(F32)
        go = g * q_all[h].astype(F32)
        hi = go.astype(BF16)
        cols = pl.ds(h * HD, HD)
        go_hi[:, cols] = hi
        go_lo[:, cols] = (go - hi.astype(F32)).astype(BF16)
        g_all[h] = (g * scale).astype(BF16)
    send_g = remote(g_all.at[pl.ds(GROUP * (1 - core), GROUP)], g_s.at[core], x_ssem.at[0], x_rsem.at[0], mate_dev)
    send_g.start()
    loads[4].wait()
    q_all[...] = jnp.swapaxes(q_in[...], 0, 1)
    send_q = remote(q_all.at[pl.ds(GROUP * (1 - core), GROUP)], q_s.at[core], x_ssem.at[1], x_rsem.at[1], mate_dev)
    send_q.start()
    g_s[core] = g_all[pl.ds(GROUP * core, GROUP)]
    q_s[core] = q_all[pl.ds(GROUP * core, GROUP)]

    big = iota((2 * GROUP * HD, HD), 0) // HD
    bl = iota((2 * GROUP * HD, HD), 1)
    pick = jnp.where((bl >= DOC_LANE) & (bl < DOC_LANE + 48) & (lax.rem(bl, 16) == big), 1.0, 0.0).astype(BF16)
    delta = dot(go_hi[...], pick, NN) + dot(go_lo[...], pick, NN)
    loads[5].wait()
    ln = ln_in[...]
    norm = jnp.concatenate([ln, ln, ln, jnp.zeros((80, TOK), F32)], axis=0).T
    z = jnp.where(lanes < 48, norm * (-(HD ** 0.5)), -(delta * scale))
    hi = z.astype(BF16)
    rest = z - hi.astype(F32)
    mid = rest.astype(BF16)
    low = (rest - mid.astype(F32)).astype(BF16)
    term = lax.rem(lanes, 64) // 16
    a_all[...] = jnp.where(term == 0, hi.astype(F32), jnp.where(term == 1, mid.astype(F32), low.astype(F32))).astype(BF16)
    send_a = remote(a_all, a_s.at[core], x_ssem.at[2], x_rsem.at[2], mate_dev)
    send_a.start()
    a_s[core] = a_all[...]

    def prepare(qb):
        a = a_s[qb].astype(F32)
        hot = one_hot(chip2 + qb)
        base = jnp.where(hot, 1.0, 0.0)
        slot = lax.rem(lanes, 16)
        for g in range(GROUP):
            mine = slot == GROUP * core + g
            xaug[qb, g] = jnp.where(mine & (lanes < 48), a, base).astype(BF16)
            yaug[qb, g] = jnp.where(mine & (lanes >= 64) & (lanes < 112), a, 0.0).astype(BF16)
            cols = pl.ds(pl.multiple_of((qb * GROUP + g) * TOK, TOK), TOK)
            qt[:, cols] = q_s[qb, g].T
            gt[:, cols] = g_s[qb, g].T

    ones = jnp.ones((TOK, HD), BF16)

    def keys_of(kbs):
        return jnp.concatenate([jnp.concatenate([kvs[kb, 0], kaug[kb]], axis=1) for kb in kbs], axis=0)

    def values_of(kbs):
        return jnp.concatenate([jnp.concatenate([kvs[kb, 1], ones], axis=1) for kb in kbs], axis=0)

    causal = iota((TOK, TOK), 0) >= iota((TOK, TOK), 1)

    def scores(qb, kbs, diagonal=False):
        width = TOK * len(kbs)
        cols = pl.ds(kbs[0] * TOK, width)
        keys, values = keys_of(kbs), values_of(kbs)
        for g in range(GROUP):
            x = jnp.concatenate([q_s[qb, g], xaug[qb, g]], axis=1)
            y = jnp.concatenate([g_s[qb, g], yaug[qb, g]], axis=1)
            p = jnp.exp(dot(x, keys, NT) * SCALE)
            if diagonal:
                keep = causal if len(kbs) == 1 else jnp.concatenate([jnp.ones((TOK, TOK), jnp.bool_), causal], axis=1)
                p = jnp.where(keep, p, 0.0)
            ds = p * dot(y, values, NT)
            at_rows = pl.ds((qb * GROUP + g) * TOK, TOK)
            p_buf[at_rows, cols] = p.astype(BF16)
            d_buf[at_rows, cols] = ds.astype(BF16)

    half = GROUP * TOK

    def kv_grads(first_row, kb, count):
        r = pl.ds(first_row, 2 * half - first_row) if first_row else slice(None)
        c = pl.ds(kb * TOK, count * TOK)
        return dot(qt[:, r], d_buf[r, c], NN), dot(gt[:, r], p_buf[r, c], NN)

    prepare(core)
    wait_block(5 - core)
    for s in (send_g, send_q, send_a):
        s.wait_recv()
    prepare(1 - core)

    scores(0, (4,), True)
    scores(1, (4, 5), True)
    dk0, dv0 = kv_grads(0, 4, 1)
    dk1, dv1 = kv_grads(half, 5, 1)
    own_part[0, 0] = dk0
    own_part[0, 1] = dv0
    own_part[1, 0] = dk1
    own_part[1, 1] = dv1
    send_m = remote(own_part.at[1 - core], mate_part, m_ssem.at[0], m_rsem.at[0], mate_dev)
    send_m.start()

    for j in (0, 1):
        wait_block(2 + j)
        onward = remote(kvs.at[2 + j], kvs.at[j], kv_ssem.at[3 + j], kv_rsem.at[j], at(1, core))
        onward.start()
        sends.append(onward)

    returns = []

    def give_back(i, j, chips, slot, dk, dv):
        ret_send[i, 0] = dk.astype(BF16)
        ret_send[i, 1] = dv.astype(BF16)
        c = remote(ret_send.at[i], ret_recv.at[slot + core], r_ssem.at[i], r_rsem.at[slot + core], at(chips, j))
        c.start()
        returns.append(c)

    scores(0, (2, 3))
    scores(1, (2, 3))
    dk, dv = kv_grads(0, 2, 2)
    for j in (0, 1):
        give_back(j, j, -1, 0, dk[:, j * TOK:(j + 1) * TOK], dv[:, j * TOK:(j + 1) * TOK])

    def query_grads(qb, first, count):
        keys = kvs[first:first + count, 0].reshape(count * TOK, HD)
        return dot(d_buf[qb * half:(qb + 1) * half, first * TOK:(first + count) * TOK], keys, NN)

    dq_acc[0] = query_grads(0, 2, 3).reshape(GROUP, TOK, HD)
    dq_acc[1] = query_grads(1, 2, 4).reshape(GROUP, TOK, HD)

    wait_block(0)
    scores(0, (0,))
    r0 = pl.ds(0, half)
    c0 = pl.ds(0, TOK)
    give_back(2, 0, -2, 2, dot(qt[:, r0], d_buf[r0, c0], NN), dot(gt[:, r0], p_buf[r0, c0], NN))
    wait_block(1)
    scores(0, (1,))
    scores(1, (1,))
    give_back(3, 1, -2, 2, *kv_grads(0, 1, 1))

    dq_acc[0] = (dq_acc[0] + query_grads(0, 0, 2).reshape(GROUP, TOK, HD)) * SCALE
    dq_acc[1] = (dq_acc[1] + query_grads(1, 1, 1).reshape(GROUP, TOK, HD)) * SCALE
    send_dq = remote(dq_acc.at[1 - core], dq_mate, dq_ssem.at[0], dq_rsem.at[0], mate_dev)
    send_dq.start()
    send_dq.wait_recv()
    low = jnp.where(core == 0, dq_acc[core], dq_mate[...])
    high = jnp.where(core == 0, dq_mate[...], dq_acc[core])
    dq_ref[:, :GROUP] = jnp.swapaxes(low, 0, 1)
    dq_ref[:, GROUP:] = jnp.swapaxes(high, 0, 1)

    send_m.wait_recv()
    for i in range(4):
        wait_return(i)

    def add_up(part, h):
        x = part + ret_recv[h].astype(F32) + ret_recv[2 + h].astype(F32)
        totals[0, h] = x[0].T * SCALE
        totals[1, h] = x[1].T

    add_up(own_part[core], core)
    add_up(mate_part[...], 1 - core)
    dk_ref[...] = jnp.swapaxes(totals[0], 0, 1)
    dv_ref[...] = jnp.swapaxes(totals[1], 0, 1)
    for s in sends + [send_g, send_q, send_a, send_m, send_dq] + returns:
        s.wait_send()


def shards(n_ctx, queries, keys, values, attn_out, grad_out, log_norm, doc_lengths, doc_weight):
    any_space = pl.BlockSpec(memory_space=pl.ANY)
    smem = pl.BlockSpec(memory_space=pltpu.SMEM)
    vmem = pl.BlockSpec(memory_space=pltpu.VMEM)
    dma = pltpu.SemaphoreType.DMA
    q_shape, k_shape = queries.shape, keys.shape
    wide = 2 * GROUP * TOK

    def buf(*shape, dtype=BF16):
        return pltpu.VMEM(shape, dtype)

    return pl.pallas_call(
        functools.partial(kernel, n_ctx),
        out_shape=(
            buf(*q_shape, dtype=F32),
            buf(*k_shape, dtype=F32),
            buf(*k_shape, dtype=F32),
        ),
        in_specs=[any_space] * 6 + [smem] * 2,
        out_specs=(vmem, vmem, vmem),
        scratch_shapes=[
            buf(*q_shape), buf(*k_shape), buf(*k_shape), buf(*q_shape), buf(*q_shape), buf(2 * GROUP, TOK, dtype=F32),
            buf(2, 2, TOK, HD), buf(6, 2, TOK, HD), buf(6, TOK, HD),
            buf(2 * GROUP, TOK, HD), buf(2 * GROUP, TOK, HD), buf(TOK, HD),
            buf(2, GROUP, TOK, HD), buf(2, GROUP, TOK, HD), buf(2, TOK, HD),
            buf(2, GROUP, TOK, HD), buf(2, GROUP, TOK, HD),
            buf(HD, wide), buf(HD, wide), buf(TOK, 2 * GROUP * HD), buf(TOK, 2 * GROUP * HD),
            buf(wide, 6 * TOK), buf(wide, 6 * TOK),
            buf(2, 2, HD, TOK, dtype=F32), buf(2, HD, TOK, dtype=F32),
            buf(4, 2, HD, TOK), buf(4, 2, HD, TOK),
            buf(2, GROUP, TOK, HD, dtype=F32), buf(GROUP, TOK, HD, dtype=F32), buf(2, 2, TOK, HD, dtype=F32),
            dma((6,)), dma((5,)), dma((6,)), dma((3,)), dma((3,)), dma((4,)), dma((4,)), dma((1,)), dma((1,)),
            dma((1,)), dma((1,)),
        ],
        compiler_params=pltpu.CompilerParams(collective_id=0, has_side_effects=True, vmem_limit_bytes=52 << 20),
    )(queries, keys, values, attn_out, grad_out, log_norm, doc_lengths, doc_weight)


def solution(mesh):
    return jax.shard_map(
        functools.partial(shards, mesh.shape["ctx"]),
        mesh=mesh,
        in_specs=(
            P("ctx", "tp", None),
            P("ctx", "tp", None),
            P("ctx", "tp", None),
            P("ctx", "tp", None),
            P("ctx", "tp", None),
            P("tp", "ctx"),
            P(),
            P(),
        ),
        out_specs=(P("ctx", "tp", None), P("ctx", "tp", None), P("ctx", "tp", None)),
        check_vma=False,
    )
```

```python
import functools

import jax
import jax.numpy as jnp
from jax import lax
from jax.experimental import pallas as pl
from jax.experimental.pallas import tpu as pltpu
from jax.sharding import PartitionSpec as P

MESH = pl.DeviceIdType.MESH
F32, BF16 = jnp.float32, jnp.bfloat16
NT = (((1,), (1,)), ((), ()))
NN = (((1,), (0,)), ((), ()))

TOK = 256
HD = 128
GROUP = 8
DOCS = 32
RING = 4
SCALE = HD ** -0.5
DOC_LANE = 64
FAR_AWAY = 16384.0


def dot(a, b, dims):
    return lax.dot_general(a, b, dims, preferred_element_type=F32)


def iota(shape, dim):
    return lax.broadcasted_iota(jnp.int32, shape, dim)


def kernel(n_ctx, q_hbm, k_hbm, v_hbm, o_hbm, g_hbm, ln_hbm, dl_ref, dw_ref, dq_ref, dk_ref, dv_ref,
           q_in, k_in, v_in, o_in, g_in, ln_in,
           kv_send, kvs, kaug, q_all, g_all, a_all, q_s, g_s, a_s, xaug, yaug, qt, gt,
           p_buf, d_buf, own_part, mate_part, ret_send, ret_recv, dq_send, dq_all, totals,
           in_sem, kv_ssem, kv_rsem, x_ssem, x_rsem, r_ssem, r_rsem, m_ssem, m_rsem, dq_ssem, dq_rsem, hop, hop_ssem, hop_rsem):
    me = lax.axis_index("ctx")
    tp = lax.axis_index("tp")
    core = lax.rem(me, 2)
    chip2 = me - core
    mate = chip2 + 1 - core
    before = {1: chip2 >= 2, 2: chip2 >= 4}
    after = {1: chip2 < n_ctx - 2, 2: chip2 < n_ctx - 4}

    chip = chip2 // 2
    base, y = chip // RING * RING, lax.rem(chip, RING)
    down, up = base + lax.rem(y + RING - 1, RING), base + lax.rem(y + 1, RING)
    origin = lax.rem(chip + n_ctx // 2 - 2, n_ctx // 2)
    relay = origin // RING * RING + lax.rem(origin + RING - 1, RING)
    hop_from_here = after[2] & (core == 1)
    hop_through_here = up + 2 < n_ctx // 2
    hop_end = lax.rem(up + 2, n_ctx // 2)

    def at(chips, j):
        return (lax.rem(chip2 + 2 * chips + j + n_ctx, n_ctx), tp)

    def remote(src, dst, ssem, rsem, dev):
        return pltpu.make_async_remote_copy(src_ref=src, dst_ref=dst, send_sem=ssem, recv_sem=rsem,
                                            device_id=dev, device_id_type=MESH)

    mate_dev = (mate, tp)
    loads = [pltpu.make_async_copy(s, d, in_sem.at[i]) for i, (s, d) in enumerate(
        [(k_hbm, k_in), (v_hbm, v_in), (g_hbm, g_in), (o_hbm, o_in), (q_hbm, q_in), (ln_hbm, ln_in)])]
    for load in loads:
        load.start()
    barrier = pltpu.get_barrier_semaphore()
    pl.semaphore_signal(barrier, inc=1, device_id=mate_dev, device_id_type=MESH)
    greeted = 1
    for chips, there in ((1, after[1]), (2, after[2]), (-1, before[1]), (-2, before[2])):
        greeted = greeted + 2 * there.astype(jnp.int32)

        @pl.when(there)
        def _():
            for j in (0, 1):
                pl.semaphore_signal(barrier, inc=1, device_id=at(chips, j), device_id_type=MESH)

    for there, devs in ((hop_from_here, [(2 * down, tp), (2 * down + 1, tp)]),
                        (hop_through_here, [(2 * up + 1, tp), (2 * hop_end + core, tp)]),
                        (before[2], [(2 * relay + core, tp)])):
        greeted = greeted + len(devs) * there.astype(jnp.int32)

        @pl.when(there)
        def _():
            for dev in devs:
                pl.semaphore_signal(barrier, inc=1, device_id=dev, device_id_type=MESH)

    loads[0].wait()
    kv_send[:, 0] = jnp.swapaxes(k_in[...], 0, 1)
    loads[1].wait()
    kv_send[:, 1] = jnp.swapaxes(v_in[...], 0, 1)
    kvs[4 + core] = kv_send[core]

    lane1 = iota((1, HD), 1)
    starts = jnp.full((1, HD), 1 << 30, jnp.int32)
    ends = jnp.zeros((1, HD), jnp.int32)
    weights = jnp.zeros((1, HD), F32)
    run = jnp.int32(0)
    total = jnp.int32(0)
    for d in range(DOCS):
        here = lane1 == DOC_LANE + d
        length = dl_ref[d]
        weight = dw_ref[d]
        starts = jnp.where(here, run, starts)
        run = run + length
        ends = jnp.where(here, run, ends)
        weights = jnp.where(here, weight.astype(F32), weights)
        total = total + length * weight

    rows = iota((TOK, HD), 0)
    lanes = iota((TOK, HD), 1)

    def one_hot(block):
        pos = block * TOK + rows
        return (pos >= starts) & (pos < ends)

    for kb in range(6):
        hot = one_hot(chip2 - 4 + kb)
        extra = jnp.where(lanes < 48, 1.0, jnp.where((lanes >= DOC_LANE) & (lanes < DOC_LANE + DOCS) & ~hot, -FAR_AWAY, 0.0))
        kaug[kb] = extra.astype(BF16)

    scale = jnp.sum(jnp.where(one_hot(me), weights, 0.0), axis=1, keepdims=True)
    scale = scale * float(n_ctx * TOK) / total.astype(F32)
    scale = jnp.broadcast_to(scale, (TOK, HD))

    loads[2].wait()
    g_all[...] = jnp.swapaxes(g_in[...], 0, 1)
    loads[3].wait()
    q_all[...] = jnp.swapaxes(o_in[...], 0, 1)
    lane_slot = jnp.where(lane1 >= DOC_LANE, lax.rem(lane1, 16), -1)
    delta = jnp.zeros((TOK, HD), F32)
    for h in range(2 * GROUP):
        g = g_all[h].astype(F32)
        summed = jnp.sum(g * q_all[h].astype(F32), axis=1, keepdims=True)
        delta = jnp.where(lane_slot == h, summed, delta)
        g_all[h] = (g * scale).astype(BF16)

    pl.semaphore_wait(barrier, greeted)

    started = []

    def start(there, copy):
        @pl.when(there)
        def _():
            copy.start()
        started.append((there, copy))

    send_kv = remote(kv_send.at[1 - core], kvs.at[4 + core], kv_ssem.at[0], kv_rsem.at[4 + core], mate_dev)
    send_kv.start()
    for h in (0, 1):
        start(after[1], remote(kv_send.at[h], kvs.at[2 + core], kv_ssem.at[1 + h], kv_rsem.at[2 + core], at(1, h)))

    def arrive(there, landed, copy):
        @pl.when(there)
        def _():
            copy.wait_recv()

        @pl.when(jnp.logical_not(there))
        def _():
            landed[...] = jnp.zeros(landed.shape, landed.dtype)

    def wait_block(kb):
        arrive(before[2 - kb // 2], kvs.at[kb],
               remote(kv_send.at[0], kvs.at[kb], kv_ssem.at[0], kv_rsem.at[kb], mate_dev))

    def wait_return(i):
        arrive(after[1 + i // 2], ret_recv.at[i],
               remote(ret_send.at[0], ret_recv.at[i], r_ssem.at[0], r_rsem.at[i], mate_dev))

    def wait_mate():
        remote(kv_send.at[0], kvs.at[5 - core], kv_ssem.at[0], kv_rsem.at[5 - core], mate_dev).wait_recv()

    for h in (0, 1):
        start(hop_from_here, remote(kv_send.at[h], hop, hop_ssem.at[h], hop_rsem.at[0], (2 * down + h, tp)))

    send_g = remote(g_all.at[pl.ds(GROUP * (1 - core), GROUP)], g_s.at[core], x_ssem.at[0], x_rsem.at[0], mate_dev)
    send_g.start()
    loads[4].wait()
    q_all[...] = jnp.swapaxes(q_in[...], 0, 1)
    send_q = remote(q_all.at[pl.ds(GROUP * (1 - core), GROUP)], q_s.at[core], x_ssem.at[1], x_rsem.at[1], mate_dev)
    send_q.start()
    g_s[core] = g_all[pl.ds(GROUP * core, GROUP)]
    q_s[core] = q_all[pl.ds(GROUP * core, GROUP)]

    loads[5].wait()
    ln = ln_in[...]
    norm = jnp.concatenate([ln, ln, ln, jnp.zeros((80, TOK), F32)], axis=0).T
    z = jnp.where(lanes < 48, norm * (-(HD ** 0.5)), -(delta * scale))
    hi = z.astype(BF16)
    rest = z - hi.astype(F32)
    mid = rest.astype(BF16)
    low = (rest - mid.astype(F32)).astype(BF16)
    term = lax.rem(lanes, 64) // 16
    a_all[...] = jnp.where(term == 0, hi.astype(F32), jnp.where(term == 1, mid.astype(F32), low.astype(F32))).astype(BF16)
    send_a = remote(a_all, a_s.at[core], x_ssem.at[2], x_rsem.at[2], mate_dev)
    send_a.start()
    a_s[core] = a_all[...]

    def prepare(qb):
        a = a_s[qb].astype(F32)
        hot = one_hot(chip2 + qb)
        base = jnp.where(hot, 1.0, 0.0)
        slot = lax.rem(lanes, 16)
        for g in range(GROUP):
            mine = slot == GROUP * core + g
            xaug[qb, g] = jnp.where(mine & (lanes < 48), a, base).astype(BF16)
            yaug[qb, g] = jnp.where(mine & (lanes >= 64) & (lanes < 112), a, 0.0).astype(BF16)
            cols = pl.ds(pl.multiple_of((qb * GROUP + g) * TOK, TOK), TOK)
            qt[:, cols] = q_s[qb, g].T
            gt[:, cols] = g_s[qb, g].T

    ones = jnp.ones((TOK, HD), BF16)

    def keys_of(kbs):
        return jnp.concatenate([jnp.concatenate([kvs[kb, 0], kaug[kb]], axis=1) for kb in kbs], axis=0)

    def values_of(kbs):
        return jnp.concatenate([jnp.concatenate([kvs[kb, 1], ones], axis=1) for kb in kbs], axis=0)

    causal = iota((TOK, TOK), 0) >= iota((TOK, TOK), 1)

    def scores(qb, kbs, diagonal=False):
        width = TOK * len(kbs)
        cols = pl.ds(kbs[0] * TOK, width)
        keys, values = keys_of(kbs), values_of(kbs)
        for g in range(GROUP):
            x = jnp.concatenate([q_s[qb, g], xaug[qb, g]], axis=1)
            y = jnp.concatenate([g_s[qb, g], yaug[qb, g]], axis=1)
            p = jnp.exp(dot(x, keys, NT) * SCALE)
            if diagonal:
                keep = causal if len(kbs) == 1 else jnp.concatenate([jnp.ones((TOK, TOK), jnp.bool_), causal], axis=1)
                p = jnp.where(keep, p, 0.0)
            ds = p * dot(y, values, NT)
            at_rows = pl.ds((qb * GROUP + g) * TOK, TOK)
            p_buf[at_rows, cols] = p.astype(BF16)
            d_buf[at_rows, cols] = ds.astype(BF16)

    half = GROUP * TOK

    def kv_grads(first_row, kb, count):
        r = pl.ds(first_row, 2 * half - first_row) if first_row else slice(None)
        c = pl.ds(kb * TOK, count * TOK)
        return dot(qt[:, r], d_buf[r, c], NN), dot(gt[:, r], p_buf[r, c], NN)

    prepare(core)
    wait_mate()
    for s in (send_g, send_q, send_a):
        s.wait_recv()
    prepare(1 - core)

    scores(0, (4,), True)

    @pl.when(hop_through_here)
    def _():
        remote(kv_send.at[0], hop, hop_ssem.at[0], hop_rsem.at[0], mate_dev).wait_recv()
    start(hop_through_here, remote(hop, kvs.at[1], kv_ssem.at[4], kv_rsem.at[1], (2 * hop_end + core, tp)))
    scores(1, (4, 5), True)
    dk0, dv0 = kv_grads(0, 4, 1)
    dk1, dv1 = kv_grads(half, 5, 1)
    own_part[0, 0] = dk0
    own_part[0, 1] = dv0
    own_part[1, 0] = dk1
    own_part[1, 1] = dv1
    send_m = remote(own_part.at[1 - core], mate_part, m_ssem.at[0], m_rsem.at[0], mate_dev)
    send_m.start()

    def pass_on(j):
        start(before[1] & after[1],
              remote(kvs.at[2 + j], kvs.at[j], kv_ssem.at[3 + j], kv_rsem.at[j], at(1, core)))

    def give_back(i, j, chips, dk, dv):
        ret_send[i, 0] = dk.astype(BF16)
        ret_send[i, 1] = dv.astype(BF16)
        slot = 2 * chips - 2 + core
        start(before[chips], remote(ret_send.at[i], ret_recv.at[slot], r_ssem.at[i], r_rsem.at[slot], at(-chips, j)))

    wait_block(2)
    pass_on(0)
    wait_block(3)
    for j in (1, 0):
        scores(0, (2 + j,))
        scores(1, (2 + j,))
        give_back(j, j, 1, *kv_grads(0, 2 + j, 1))

    wait_block(1)
    scores(0, (1,))
    scores(1, (1,))
    give_back(3, 1, 2, *kv_grads(0, 1, 1))
    wait_block(0)
    scores(0, (0,))
    r0 = pl.ds(0, half)
    c0 = pl.ds(0, TOK)
    give_back(2, 0, 2, dot(qt[:, r0], d_buf[r0, c0], NN), dot(gt[:, r0], p_buf[r0, c0], NN))

    def query_grads(qb):
        keys = kvs[pl.ds(qb, 5), 0].reshape(5 * TOK, HD)
        r = pl.ds(pl.multiple_of(qb * half, half), half)
        c = pl.ds(pl.multiple_of(qb * TOK, TOK), 5 * TOK)
        return (dot(d_buf[r, c], keys, NN) * SCALE).reshape(GROUP, TOK, HD)

    dq_send[...] = query_grads(1 - core)
    send_dq = remote(dq_send, dq_all.at[pl.ds(GROUP * core, GROUP)], dq_ssem.at[0], dq_rsem.at[0], mate_dev)
    send_dq.start()
    dq_all[pl.ds(GROUP * core, GROUP)] = query_grads(core)
    send_dq.wait_recv()
    dq_ref[...] = jnp.swapaxes(dq_all[...], 0, 1)

    send_m.wait_recv()
    for i in range(4):
        wait_return(i)

    def add_up(part, h):
        x = part + ret_recv[h].astype(F32) + ret_recv[2 + h].astype(F32)
        totals[0, h] = x[0].T * SCALE
        totals[1, h] = x[1].T

    add_up(own_part[core], core)
    add_up(mate_part[...], 1 - core)
    dk_ref[...] = jnp.swapaxes(totals[0], 0, 1)
    dv_ref[...] = jnp.swapaxes(totals[1], 0, 1)
    for s in (send_kv, send_g, send_q, send_a, send_m, send_dq):
        s.wait_send()
    for there, copy in started:
        pl.when(there)(copy.wait_send)


def shards(n_ctx, queries, keys, values, attn_out, grad_out, log_norm, doc_lengths, doc_weight):
    any_space = pl.BlockSpec(memory_space=pl.ANY)
    smem = pl.BlockSpec(memory_space=pltpu.SMEM)
    vmem = pl.BlockSpec(memory_space=pltpu.VMEM)
    dma = pltpu.SemaphoreType.DMA
    q_shape, k_shape = queries.shape, keys.shape
    wide = 2 * GROUP * TOK

    def buf(*shape, dtype=BF16):
        return pltpu.VMEM(shape, dtype)

    return pl.pallas_call(
        functools.partial(kernel, n_ctx),
        out_shape=(
            buf(*q_shape, dtype=F32),
            buf(*k_shape, dtype=F32),
            buf(*k_shape, dtype=F32),
        ),
        in_specs=[any_space] * 6 + [smem] * 2,
        out_specs=(vmem, vmem, vmem),
        scratch_shapes=[
            buf(*q_shape), buf(*k_shape), buf(*k_shape), buf(*q_shape), buf(*q_shape), buf(2 * GROUP, TOK, dtype=F32),
            buf(2, 2, TOK, HD), buf(6, 2, TOK, HD), buf(6, TOK, HD),
            buf(2 * GROUP, TOK, HD), buf(2 * GROUP, TOK, HD), buf(TOK, HD),
            buf(2, GROUP, TOK, HD), buf(2, GROUP, TOK, HD), buf(2, TOK, HD),
            buf(2, GROUP, TOK, HD), buf(2, GROUP, TOK, HD),
            buf(HD, wide), buf(HD, wide),
            buf(wide, 6 * TOK), buf(wide, 6 * TOK),
            buf(2, 2, HD, TOK, dtype=F32), buf(2, HD, TOK, dtype=F32),
            buf(4, 2, HD, TOK), buf(4, 2, HD, TOK),
            buf(GROUP, TOK, HD, dtype=F32), buf(2 * GROUP, TOK, HD, dtype=F32), buf(2, 2, TOK, HD, dtype=F32),
            dma((6,)), dma((5,)), dma((6,)), dma((3,)), dma((3,)), dma((4,)), dma((4,)), dma((1,)), dma((1,)),
            dma((1,)), dma((1,)), buf(2, TOK, HD), dma((2,)), dma((1,)),
        ],
        compiler_params=pltpu.CompilerParams(collective_id=0, has_side_effects=True, vmem_limit_bytes=52 << 20),
    )(queries, keys, values, attn_out, grad_out, log_norm, doc_lengths, doc_weight)


def solution(mesh):
    return jax.shard_map(
        functools.partial(shards, mesh.shape["ctx"]),
        mesh=mesh,
        in_specs=(
            P("ctx", "tp", None),
            P("ctx", "tp", None),
            P("ctx", "tp", None),
            P("ctx", "tp", None),
            P("ctx", "tp", None),
            P("tp", "ctx"),
            P(),
            P(),
        ),
        out_specs=(P("ctx", "tp", None), P("ctx", "tp", None), P("ctx", "tp", None)),
        check_vma=False,
    )
```

```python
import functools

import jax
import jax.numpy as jnp
from jax import lax
from jax.experimental import pallas as pl
from jax.experimental.pallas import tpu as pltpu
from jax.sharding import PartitionSpec as P

MESH = pl.DeviceIdType.MESH
F32, BF16 = jnp.float32, jnp.bfloat16
NT = (((1,), (1,)), ((), ()))
NN = (((1,), (0,)), ((), ()))

TOK = 256
HD = 128
GROUP = 8
DOCS = 32
RING = 4
PIECES = 2
SCALE = HD ** -0.5
DOC_LANE = 64
FAR_AWAY = 16384.0


def dot(a, b, dims):
    return lax.dot_general(a, b, dims, preferred_element_type=F32)


def iota(shape, dim):
    return lax.broadcasted_iota(jnp.int32, shape, dim)


def kernel(n_ctx, q_hbm, k_hbm, v_hbm, o_hbm, g_hbm, ln_hbm, dl_ref, dw_ref, dq_ref, dkv_ref,
           q_in, k_in, v_in, o_in, g_in, ln_in,
           kv_send, kvs, kaug, q_all, g_all, a_all, q_s, g_s, a_s, xaug, yaug, qt, gt,
           p_buf, d_buf, own_part, mate_part, ret_send, ret_recv, dq_send, dq_recv, totals,
           in_sem, kv_ssem, kv_rsem, x_ssem, x_rsem, r_ssem, r_rsem, m_ssem, m_rsem, dq_ssem, dq_rsem, hop, hop_ssem, hop_rsem):
    me = lax.axis_index("ctx")
    tp = lax.axis_index("tp")
    core = lax.rem(me, 2)
    chip2 = me - core
    mate = chip2 + 1 - core
    before = {1: chip2 >= 2, 2: chip2 >= 4}
    after = {1: chip2 < n_ctx - 2, 2: chip2 < n_ctx - 4}

    chip = chip2 // 2
    base, y = chip // RING * RING, lax.rem(chip, RING)
    down, up = base + lax.rem(y + RING - 1, RING), base + lax.rem(y + 1, RING)
    origin = lax.rem(chip + n_ctx // 2 - 2, n_ctx // 2)
    relay = origin // RING * RING + lax.rem(origin + RING - 1, RING)
    hop_from_here = after[2] & (core == 1)
    hop_through_here = up + 2 < n_ctx // 2
    hop_end = lax.rem(up + 2, n_ctx // 2)

    def at(chips, j):
        return (lax.rem(chip2 + 2 * chips + j + n_ctx, n_ctx), tp)

    def remote(src, dst, ssem, rsem, dev):
        return pltpu.make_async_remote_copy(src_ref=src, dst_ref=dst, send_sem=ssem, recv_sem=rsem,
                                            device_id=dev, device_id_type=MESH)

    mate_dev = (mate, tp)
    loads = [pltpu.make_async_copy(s, d, in_sem.at[i]) for i, (s, d) in enumerate(
        [(k_hbm, k_in), (v_hbm, v_in), (g_hbm, g_in), (o_hbm, o_in), (q_hbm, q_in), (ln_hbm, ln_in)])]
    loads[0].start()
    loads[1].start()
    barrier = pltpu.get_barrier_semaphore()
    pl.semaphore_signal(barrier, inc=1, device_id=mate_dev, device_id_type=MESH)
    greeted = 1
    for chips, there in ((1, after[1]), (2, after[2]), (-1, before[1]), (-2, before[2])):
        greeted = greeted + 2 * there.astype(jnp.int32)

        @pl.when(there)
        def _():
            for j in (0, 1):
                pl.semaphore_signal(barrier, inc=1, device_id=at(chips, j), device_id_type=MESH)

    for there, devs in ((hop_from_here, [(2 * down, tp), (2 * down + 1, tp)]),
                        (hop_through_here, [(2 * up + 1, tp), (2 * hop_end + core, tp)]),
                        (before[2], [(2 * relay + core, tp)])):
        greeted = greeted + len(devs) * there.astype(jnp.int32)

        @pl.when(there)
        def _():
            for dev in devs:
                pl.semaphore_signal(barrier, inc=1, device_id=dev, device_id_type=MESH)

    for load in loads[2:]:
        load.start()
    loads[0].wait()
    kv_send[:, 0] = jnp.swapaxes(k_in[...], 0, 1)
    loads[1].wait()
    kv_send[:, 1] = jnp.swapaxes(v_in[...], 0, 1)
    kvs[4 + core] = kv_send[core]

    lane1 = iota((1, HD), 1)
    starts = jnp.full((1, HD), 1 << 30, jnp.int32)
    ends = jnp.zeros((1, HD), jnp.int32)
    weights = jnp.zeros((1, HD), F32)
    run = jnp.int32(0)
    total = jnp.int32(0)
    for d in range(DOCS):
        here = lane1 == DOC_LANE + d
        length = dl_ref[d]
        weight = dw_ref[d]
        starts = jnp.where(here, run, starts)
        run = run + length
        ends = jnp.where(here, run, ends)
        weights = jnp.where(here, weight.astype(F32), weights)
        total = total + length * weight

    rows = iota((TOK, HD), 0)
    lanes = iota((TOK, HD), 1)

    def one_hot(block):
        pos = block * TOK + rows
        return (pos >= starts) & (pos < ends)

    for kb in range(6):
        hot = one_hot(chip2 - 4 + kb)
        extra = jnp.where(lanes < 48, 1.0, jnp.where((lanes >= DOC_LANE) & (lanes < DOC_LANE + DOCS) & ~hot, -FAR_AWAY, 0.0))
        kaug[kb] = extra.astype(BF16)

    scale = jnp.sum(jnp.where(one_hot(me), weights, 0.0), axis=1, keepdims=True)
    scale = scale * float(n_ctx * TOK) / total.astype(F32)
    scale = jnp.broadcast_to(scale, (TOK, HD))

    loads[2].wait()
    g_all[...] = jnp.swapaxes(g_in[...], 0, 1)
    loads[3].wait()
    q_all[...] = jnp.swapaxes(o_in[...], 0, 1)
    lane_slot = jnp.where(lane1 >= DOC_LANE, lax.rem(lane1, 16), -1)
    delta = jnp.zeros((TOK, HD), F32)
    for h in range(2 * GROUP):
        g = g_all[h].astype(F32)
        summed = jnp.sum(g * q_all[h].astype(F32), axis=1, keepdims=True)
        delta = jnp.where(lane_slot == h, summed, delta)
        g_all[h] = (g * scale).astype(BF16)

    pl.semaphore_wait(barrier, greeted)

    started = []

    def start(there, copy):
        @pl.when(there)
        def _():
            copy.start()
        started.append((there, copy))

    send_kv = remote(kv_send.at[1 - core], kvs.at[4 + core], kv_ssem.at[0], kv_rsem.at[4 + core], mate_dev)
    send_kv.start()

    def send_near(j):
        for h in (0, 1):
            start(after[1] & (core == j),
                  remote(kv_send.at[h], kvs.at[2 + core], kv_ssem.at[1 + h], kv_rsem.at[2 + core], at(1, h)))

    send_near(0)

    def arrive(there, landed, copy):
        @pl.when(there)
        def _():
            copy.wait_recv()

        @pl.when(jnp.logical_not(there))
        def _():
            landed[...] = jnp.zeros(landed.shape, landed.dtype)

    def wait_block(kb):
        arrive(before[2 - kb // 2], kvs.at[kb],
               remote(kv_send.at[0], kvs.at[kb], kv_ssem.at[0], kv_rsem.at[kb], mate_dev))

    def wait_return(i):
        arrive(after[1 + i // 2], ret_recv.at[i],
               remote(ret_send.at[0], ret_recv.at[i], r_ssem.at[0], r_rsem.at[i], mate_dev))

    def wait_mate():
        remote(kv_send.at[0], kvs.at[5 - core], kv_ssem.at[0], kv_rsem.at[5 - core], mate_dev).wait_recv()

    for h in (0, 1):
        start(hop_from_here, remote(kv_send.at[h], hop, hop_ssem.at[h], hop_rsem.at[0], (2 * down + h, tp)))

    send_g = remote(g_all.at[pl.ds(GROUP * (1 - core), GROUP)], g_s.at[core], x_ssem.at[0], x_rsem.at[0], mate_dev)
    send_g.start()
    loads[4].wait()
    q_all[...] = jnp.swapaxes(q_in[...], 0, 1)
    send_q = remote(q_all.at[pl.ds(GROUP * (1 - core), GROUP)], q_s.at[core], x_ssem.at[1], x_rsem.at[1], mate_dev)
    send_q.start()
    g_s[core] = g_all[pl.ds(GROUP * core, GROUP)]
    q_s[core] = q_all[pl.ds(GROUP * core, GROUP)]

    loads[5].wait()
    ln = ln_in[...]
    norm = jnp.concatenate([ln, ln, ln, jnp.zeros((80, TOK), F32)], axis=0).T
    z = jnp.where(lanes < 48, norm * (-(HD ** 0.5)), -(delta * scale))
    hi = z.astype(BF16)
    rest = z - hi.astype(F32)
    mid = rest.astype(BF16)
    low = (rest - mid.astype(F32)).astype(BF16)
    term = lax.rem(lanes, 64) // 16
    a_all[...] = jnp.where(term == 0, hi.astype(F32), jnp.where(term == 1, mid.astype(F32), low.astype(F32))).astype(BF16)
    send_a = remote(a_all, a_s.at[core], x_ssem.at[2], x_rsem.at[2], mate_dev)
    send_a.start()
    a_s[core] = a_all[...]

    def prepare(qb):
        a = a_s[qb].astype(F32)
        hot = one_hot(chip2 + qb)
        base = jnp.where(hot, 1.0, 0.0)
        slot = lax.rem(lanes, 16)
        for g in range(GROUP):
            mine = slot == GROUP * core + g
            xaug[qb, g] = jnp.where(mine & (lanes < 48), a, base).astype(BF16)
            yaug[qb, g] = jnp.where(mine & (lanes >= 64) & (lanes < 112), a, 0.0).astype(BF16)
            cols = pl.ds(pl.multiple_of((qb * GROUP + g) * TOK, TOK), TOK)
            qt[:, cols] = q_s[qb, g].T
            gt[:, cols] = g_s[qb, g].T

    ones = jnp.ones((TOK, HD), BF16)

    def keys_of(kbs):
        return jnp.concatenate([jnp.concatenate([kvs[kb, 0], kaug[kb]], axis=1) for kb in kbs], axis=0)

    def values_of(kbs):
        return jnp.concatenate([jnp.concatenate([kvs[kb, 1], ones], axis=1) for kb in kbs], axis=0)

    causal = iota((TOK, TOK), 0) >= iota((TOK, TOK), 1)

    def scores(qb, kbs, diagonal=False):
        width = TOK * len(kbs)
        cols = pl.ds(pl.multiple_of(kbs[0] * TOK, TOK), width)
        keys, values = keys_of(kbs), values_of(kbs)
        for g in range(GROUP):
            x = jnp.concatenate([q_s[qb, g], xaug[qb, g]], axis=1)
            y = jnp.concatenate([g_s[qb, g], yaug[qb, g]], axis=1)
            p = jnp.exp(dot(x, keys, NT) * SCALE)
            if diagonal:
                p = jnp.where(causal, p, 0.0)
            ds = p * dot(y, values, NT)
            at_rows = pl.ds(pl.multiple_of((qb * GROUP + g) * TOK, TOK), TOK)
            p_buf[at_rows, cols] = p.astype(BF16)
            d_buf[at_rows, cols] = ds.astype(BF16)

    half = GROUP * TOK

    def kv_grads(first_row, kb, count):
        r = pl.ds(first_row, 2 * half - first_row) if first_row else slice(None)
        c = pl.ds(kb * TOK, count * TOK)
        return dot(qt[:, r], d_buf[r, c], NN), dot(gt[:, r], p_buf[r, c], NN)

    prepare(core)
    scores(core, (4 + core,), True)
    wait_mate()
    for s in (send_g, send_q, send_a):
        s.wait_recv()
    prepare(1 - core)
    send_near(1)

    scores(1 - core, (5 - core,), True)
    scores(1, (4,))

    @pl.when(hop_through_here)
    def _():
        remote(kv_send.at[0], hop, hop_ssem.at[0], hop_rsem.at[0], mate_dev).wait_recv()
    start(hop_through_here, remote(hop, kvs.at[1], kv_ssem.at[4], kv_rsem.at[1], (2 * hop_end + core, tp)))

    def own_grads(j):
        dk, dv = kv_grads(j * half, 4 + j, 1)
        own_part[j, 0] = dk
        own_part[j, 1] = dv

    own_grads(0)

    def pass_on(j):
        start(before[1] & after[1],
              remote(kvs.at[2 + j], kvs.at[j], kv_ssem.at[3 + j], kv_rsem.at[j], at(1, core)))

    def give_back(i, j, chips, dk, dv):
        ret_send[i, 0] = dk.astype(BF16)
        ret_send[i, 1] = dv.astype(BF16)
        slot = 2 * chips - 2 + core
        start(before[chips], remote(ret_send.at[i], ret_recv.at[slot], r_ssem.at[i], r_rsem.at[slot], at(-chips, j)))

    send_m = remote(own_part.at[1 - core], mate_part, m_ssem.at[0], m_rsem.at[0], mate_dev)
    for j in (0, 1):
        wait_block(2 + j)
        if j == 0:
            pass_on(0)
        scores(0, (2 + j,))
        scores(1, (2 + j,))
        give_back(j, j, 1, *kv_grads(0, 2 + j, 1))

    wait_block(1)
    scores(0, (1,))
    scores(1, (1,))
    give_back(3, 1, 2, *kv_grads(0, 1, 1))
    wait_block(0)
    scores(0, (0,))
    r0 = pl.ds(0, half)
    c0 = pl.ds(0, TOK)
    give_back(2, 0, 2, dot(qt[:, r0], d_buf[r0, c0], NN), dot(gt[:, r0], p_buf[r0, c0], NN))

    def query_grads(qb, i):
        keys = kvs[pl.ds(qb, 5), 0].reshape(5 * TOK, HD)
        r = pl.ds(pl.multiple_of(qb * half + i * (half // PIECES), half // PIECES), half // PIECES)
        c = pl.ds(pl.multiple_of(qb * TOK, TOK), 5 * TOK)
        return (dot(d_buf[r, c], keys, NN) * SCALE).reshape(GROUP // PIECES, TOK, HD)

    sends_dq = []
    for i in range(PIECES):
        dq_send[i] = query_grads(1 - core, i)
        c = remote(dq_send.at[i], dq_recv.at[i], dq_ssem.at[i], dq_rsem.at[i], mate_dev)
        c.start()
        sends_dq.append(c)
    own_grads(1)
    send_m.start()

    def put(group, x):
        dq_ref[:, pl.ds(pl.multiple_of(GROUP * group, GROUP), GROUP)] = jnp.swapaxes(x, 0, 1)

    put(core, jnp.concatenate([query_grads(core, i) for i in range(PIECES)], axis=0))
    for c in sends_dq:
        c.wait_recv()
    put(1 - core, dq_recv[...].reshape(GROUP, TOK, HD))

    send_m.wait_recv()
    for i in range(4):
        wait_return(i)

    def add_up(part, h):
        x = part + ret_recv[h].astype(F32) + ret_recv[2 + h].astype(F32)
        totals[0, h] = x[0].T * SCALE
        totals[1, h] = x[1].T

    add_up(own_part[core], core)
    add_up(mate_part[...], 1 - core)
    dkv_ref[0] = jnp.swapaxes(totals[0], 0, 1)
    dkv_ref[1] = jnp.swapaxes(totals[1], 0, 1)
    for s in [send_kv, send_g, send_q, send_a, send_m] + sends_dq:
        s.wait_send()
    for there, copy in started:
        pl.when(there)(copy.wait_send)


def shards(n_ctx, queries, keys, values, attn_out, grad_out, log_norm, doc_lengths, doc_weight):
    any_space = pl.BlockSpec(memory_space=pl.ANY)
    smem = pl.BlockSpec(memory_space=pltpu.SMEM)
    vmem = pl.BlockSpec(memory_space=pltpu.VMEM)
    dma = pltpu.SemaphoreType.DMA
    q_shape, k_shape = queries.shape, keys.shape
    wide = 2 * GROUP * TOK

    def buf(*shape, dtype=BF16):
        return pltpu.VMEM(shape, dtype)

    dq, dkv = pl.pallas_call(
        functools.partial(kernel, n_ctx),
        out_shape=(
            buf(*q_shape, dtype=F32),
            buf(2, *k_shape, dtype=F32),
        ),
        in_specs=[any_space] * 6 + [smem] * 2,
        out_specs=(vmem, vmem),
        scratch_shapes=[
            buf(*q_shape), buf(*k_shape), buf(*k_shape), buf(*q_shape), buf(*q_shape), buf(2 * GROUP, TOK, dtype=F32),
            buf(2, 2, TOK, HD), buf(6, 2, TOK, HD), buf(6, TOK, HD),
            buf(2 * GROUP, TOK, HD), buf(2 * GROUP, TOK, HD), buf(TOK, HD),
            buf(2, GROUP, TOK, HD), buf(2, GROUP, TOK, HD), buf(2, TOK, HD),
            buf(2, GROUP, TOK, HD), buf(2, GROUP, TOK, HD),
            buf(HD, wide), buf(HD, wide),
            buf(wide, 6 * TOK), buf(wide, 6 * TOK),
            buf(2, 2, HD, TOK, dtype=F32), buf(2, HD, TOK, dtype=F32),
            buf(4, 2, HD, TOK), buf(4, 2, HD, TOK),
            buf(PIECES, GROUP // PIECES, TOK, HD, dtype=F32), buf(PIECES, GROUP // PIECES, TOK, HD, dtype=F32),
            buf(2, 2, TOK, HD, dtype=F32),
            dma((6,)), dma((5,)), dma((6,)), dma((3,)), dma((3,)), dma((4,)), dma((4,)), dma((1,)), dma((1,)),
            dma((PIECES,)), dma((PIECES,)), buf(2, TOK, HD), dma((2,)), dma((1,)),
        ],
        compiler_params=pltpu.CompilerParams(collective_id=0, has_side_effects=True, vmem_limit_bytes=52 << 20),
    )(queries, keys, values, attn_out, grad_out, log_norm, doc_lengths, doc_weight)
    return dq, dkv[0], dkv[1]


def solution(mesh):
    return jax.shard_map(
        functools.partial(shards, mesh.shape["ctx"]),
        mesh=mesh,
        in_specs=(
            P("ctx", "tp", None),
            P("ctx", "tp", None),
            P("ctx", "tp", None),
            P("ctx", "tp", None),
            P("ctx", "tp", None),
            P("tp", "ctx"),
            P(),
            P(),
        ),
        out_specs=(P("ctx", "tp", None), P("ctx", "tp", None), P("ctx", "tp", None)),
        check_vma=False,
    )
```

```python
import functools

import jax
import jax.numpy as jnp
from jax import lax
from jax.experimental import pallas as pl
from jax.experimental.pallas import tpu as pltpu
from jax.sharding import PartitionSpec as P

MESH = pl.DeviceIdType.MESH
F32, BF16 = jnp.float32, jnp.bfloat16
NT = (((1,), (1,)), ((), ()))
NN = (((1,), (0,)), ((), ()))

TOK = 256
HD = 128
GROUP = 8
DOCS = 32
RING = 4
PIECES = 2
SCALE = HD ** -0.5
DOC_LANE = 64
FAR_AWAY = 16384.0


def dot(a, b, dims):
    return lax.dot_general(a, b, dims, preferred_element_type=F32)


def iota(shape, dim):
    return lax.broadcasted_iota(jnp.int32, shape, dim)


def kernel(n_ctx, q_hbm, k_hbm, v_hbm, o_hbm, g_hbm, ln_hbm, dl_ref, dw_ref, dq_ref, dkv_ref,
           q_in, k_in, v_in, o_in, g_in, ln_in,
           kv_send, kvs, kaug, q_all, g_all, a_all, q_s, g_s, a_s, xaug, yaug, qt, gt,
           p_buf, d_buf, own_part, mate_part, ret_send, ret_recv, dq_send, dq_recv, totals,
           in_sem, kv_ssem, kv_rsem, x_ssem, x_rsem, r_ssem, r_rsem, m_ssem, m_rsem, dq_ssem, dq_rsem, hop, hop_ssem, hop_rsem):
    me = lax.axis_index("ctx")
    tp = lax.axis_index("tp")
    core = lax.rem(me, 2)
    chip2 = me - core
    mate = chip2 + 1 - core
    before = {1: chip2 >= 2, 2: chip2 >= 4}
    after = {1: chip2 < n_ctx - 2, 2: chip2 < n_ctx - 4}

    chip = chip2 // 2
    base, y = chip // RING * RING, lax.rem(chip, RING)
    down, up = base + lax.rem(y + RING - 1, RING), base + lax.rem(y + 1, RING)
    origin = lax.rem(chip + n_ctx // 2 - 2, n_ctx // 2)
    relay = origin // RING * RING + lax.rem(origin + RING - 1, RING)
    hop_from_here = after[2] & (core == 1)
    hop_through_here = up + 2 < n_ctx // 2
    hop_end = lax.rem(up + 2, n_ctx // 2)

    def at(chips, j):
        return (lax.rem(chip2 + 2 * chips + j + n_ctx, n_ctx), tp)

    def remote(src, dst, ssem, rsem, dev):
        return pltpu.make_async_remote_copy(src_ref=src, dst_ref=dst, send_sem=ssem, recv_sem=rsem,
                                            device_id=dev, device_id_type=MESH)

    mate_dev = (mate, tp)
    loads = [pltpu.make_async_copy(s, d, in_sem.at[i]) for i, (s, d) in enumerate(
        [(k_hbm, k_in), (v_hbm, v_in), (g_hbm, g_in), (o_hbm, o_in), (q_hbm, q_in), (ln_hbm, ln_in)])]
    loads[0].start()
    loads[1].start()
    barrier = pltpu.get_barrier_semaphore()
    pl.semaphore_signal(barrier, inc=1, device_id=mate_dev, device_id_type=MESH)
    greeted = 1
    for chips, there in ((1, after[1]), (2, after[2]), (-1, before[1]), (-2, before[2])):
        greeted = greeted + 2 * there.astype(jnp.int32)

        @pl.when(there)
        def _():
            for j in (0, 1):
                pl.semaphore_signal(barrier, inc=1, device_id=at(chips, j), device_id_type=MESH)

    for there, devs in ((hop_from_here, [(2 * down, tp), (2 * down + 1, tp)]),
                        (hop_through_here, [(2 * up + 1, tp), (2 * hop_end + core, tp)]),
                        (before[2], [(2 * relay + core, tp)])):
        greeted = greeted + len(devs) * there.astype(jnp.int32)

        @pl.when(there)
        def _():
            for dev in devs:
                pl.semaphore_signal(barrier, inc=1, device_id=dev, device_id_type=MESH)

    for load in loads[2:]:
        load.start()
    loads[0].wait()
    kv_send[:, 0] = jnp.swapaxes(k_in[...], 0, 1)
    loads[1].wait()
    kv_send[:, 1] = jnp.swapaxes(v_in[...], 0, 1)
    kvs[4 + core] = kv_send[core]

    lane1 = iota((1, HD), 1)
    starts = jnp.full((1, HD), 1 << 30, jnp.int32)
    ends = jnp.zeros((1, HD), jnp.int32)
    weights = jnp.zeros((1, HD), F32)
    run = jnp.int32(0)
    total = jnp.int32(0)
    for d in range(DOCS):
        here = lane1 == DOC_LANE + d
        length = dl_ref[d]
        weight = dw_ref[d]
        starts = jnp.where(here, run, starts)
        run = run + length
        ends = jnp.where(here, run, ends)
        weights = jnp.where(here, weight.astype(F32), weights)
        total = total + length * weight

    rows = iota((TOK, HD), 0)
    lanes = iota((TOK, HD), 1)

    def one_hot(block):
        pos = block * TOK + rows
        return (pos >= starts) & (pos < ends)

    for kb in range(6):
        hot = one_hot(chip2 - 4 + kb)
        extra = jnp.where(lanes < 48, 1.0, jnp.where((lanes >= DOC_LANE) & (lanes < DOC_LANE + DOCS) & ~hot, -FAR_AWAY, 0.0))
        kaug[kb] = extra.astype(BF16)

    scale = jnp.sum(jnp.where(one_hot(me), weights, 0.0), axis=1, keepdims=True)
    scale = scale * float(n_ctx * TOK) / total.astype(F32)
    scale = jnp.broadcast_to(scale, (TOK, HD))

    loads[2].wait()
    g_all[...] = jnp.swapaxes(g_in[...], 0, 1)
    loads[3].wait()
    q_all[...] = jnp.swapaxes(o_in[...], 0, 1)
    lane_slot = jnp.where(lane1 >= DOC_LANE, lax.rem(lane1, 16), -1)
    delta = jnp.zeros((TOK, HD), F32)
    for h in range(2 * GROUP):
        g = g_all[h].astype(F32)
        summed = jnp.sum(g * q_all[h].astype(F32), axis=1, keepdims=True)
        delta = jnp.where(lane_slot == h, summed, delta)
        g_all[h] = (g * scale).astype(BF16)

    pl.semaphore_wait(barrier, greeted)

    started = []

    def start(there, copy):
        @pl.when(there)
        def _():
            copy.start()
        started.append((there, copy))

    send_kv = remote(kv_send.at[1 - core], kvs.at[4 + core], kv_ssem.at[0], kv_rsem.at[4 + core], mate_dev)
    send_kv.start()

    def send_near(j):
        for h in (0, 1):
            start(after[1] & (core == j),
                  remote(kv_send.at[h], kvs.at[2 + core], kv_ssem.at[1 + h], kv_rsem.at[2 + core], at(1, h)))

    send_near(0)

    def arrive(there, landed, copy):
        @pl.when(there)
        def _():
            copy.wait_recv()

        @pl.when(jnp.logical_not(there))
        def _():
            landed[...] = jnp.zeros(landed.shape, landed.dtype)

    def wait_block(kb):
        arrive(before[2 - kb // 2], kvs.at[kb],
               remote(kv_send.at[0], kvs.at[kb], kv_ssem.at[0], kv_rsem.at[kb], mate_dev))

    def wait_return(i):
        arrive(after[1 + i // 2], ret_recv.at[i],
               remote(ret_send.at[0], ret_recv.at[i], r_ssem.at[0], r_rsem.at[i], mate_dev))

    def wait_mate():
        remote(kv_send.at[0], kvs.at[5 - core], kv_ssem.at[0], kv_rsem.at[5 - core], mate_dev).wait_recv()

    for h in (0, 1):
        start(hop_from_here, remote(kv_send.at[h], hop, hop_ssem.at[h], hop_rsem.at[0], (2 * down + h, tp)))

    send_g = remote(g_all.at[pl.ds(GROUP * (1 - core), GROUP)], g_s.at[core], x_ssem.at[0], x_rsem.at[0], mate_dev)
    send_g.start()
    loads[4].wait()
    q_all[...] = jnp.swapaxes(q_in[...], 0, 1)
    send_q = remote(q_all.at[pl.ds(GROUP * (1 - core), GROUP)], q_s.at[core], x_ssem.at[1], x_rsem.at[1], mate_dev)
    send_q.start()
    g_s[core] = g_all[pl.ds(GROUP * core, GROUP)]
    q_s[core] = q_all[pl.ds(GROUP * core, GROUP)]

    loads[5].wait()
    ln = ln_in[...]
    norm = jnp.concatenate([ln, ln, ln, jnp.zeros((80, TOK), F32)], axis=0).T
    z = jnp.where(lanes < 48, norm * (-(HD ** 0.5)), -(delta * scale))
    hi = z.astype(BF16)
    rest = z - hi.astype(F32)
    mid = rest.astype(BF16)
    low = (rest - mid.astype(F32)).astype(BF16)
    term = lax.rem(lanes, 64) // 16
    a_all[...] = jnp.where(term == 0, hi.astype(F32), jnp.where(term == 1, mid.astype(F32), low.astype(F32))).astype(BF16)
    send_a = remote(a_all, a_s.at[core], x_ssem.at[2], x_rsem.at[2], mate_dev)
    send_a.start()
    a_s[core] = a_all[...]

    def prepare(qb):
        a = a_s[qb].astype(F32)
        hot = one_hot(chip2 + qb)
        base = jnp.where(hot, 1.0, 0.0)
        slot = lax.rem(lanes, 16)
        for g in range(GROUP):
            mine = slot == GROUP * core + g
            xaug[qb, g] = jnp.where(mine & (lanes < 48), a, base).astype(BF16)
            yaug[qb, g] = jnp.where(mine & (lanes >= 64) & (lanes < 112), a, 0.0).astype(BF16)
            cols = pl.ds(pl.multiple_of((qb * GROUP + g) * TOK, TOK), TOK)
            qt[:, cols] = q_s[qb, g].T
            gt[:, cols] = g_s[qb, g].T

    ones = jnp.ones((TOK, HD), BF16)

    def keys_of(kbs):
        return jnp.concatenate([jnp.concatenate([kvs[kb, 0], kaug[kb]], axis=1) for kb in kbs], axis=0)

    def values_of(kbs):
        return jnp.concatenate([jnp.concatenate([kvs[kb, 1], ones], axis=1) for kb in kbs], axis=0)

    causal = iota((TOK, TOK), 0) >= iota((TOK, TOK), 1)

    def scores(qb, kbs, diagonal=False):
        width = TOK * len(kbs)
        cols = pl.ds(pl.multiple_of(kbs[0] * TOK, TOK), width)
        keys, values = keys_of(kbs), values_of(kbs)
        for g in range(GROUP):
            x = jnp.concatenate([q_s[qb, g], xaug[qb, g]], axis=1)
            y = jnp.concatenate([g_s[qb, g], yaug[qb, g]], axis=1)
            p = jnp.exp(dot(x, keys, NT) * SCALE)
            if diagonal:
                p = jnp.where(causal, p, 0.0)
            ds = p * dot(y, values, NT)
            at_rows = pl.ds(pl.multiple_of((qb * GROUP + g) * TOK, TOK), TOK)
            p_buf[at_rows, cols] = p.astype(BF16)
            d_buf[at_rows, cols] = ds.astype(BF16)

    half = GROUP * TOK

    def kv_grads(first_row, kb, count):
        r = pl.ds(first_row, 2 * half - first_row) if first_row else slice(None)
        c = pl.ds(kb * TOK, count * TOK)
        return dot(qt[:, r], d_buf[r, c], NN), dot(gt[:, r], p_buf[r, c], NN)

    prepare(core)
    scores(core, (4 + core,), True)
    wait_mate()
    for s in (send_g, send_q, send_a):
        s.wait_recv()
    prepare(1 - core)
    send_near(1)

    scores(1 - core, (5 - core,), True)
    scores(1, (4,))

    @pl.when(hop_through_here)
    def _():
        remote(kv_send.at[0], hop, hop_ssem.at[0], hop_rsem.at[0], mate_dev).wait_recv()
    start(hop_through_here, remote(hop, kvs.at[1], kv_ssem.at[4], kv_rsem.at[1], (2 * hop_end + core, tp)))

    def own_grads(j):
        dk, dv = kv_grads(j * half, 4 + j, 1)
        own_part[j, 0] = dk
        own_part[j, 1] = dv

    own_grads(0)

    def pass_on(j):
        start(before[1] & after[1],
              remote(kvs.at[2 + j], kvs.at[j], kv_ssem.at[3 + j], kv_rsem.at[j], at(1, core)))

    def give_back(i, j, chips, dk, dv):
        ret_send[i, 0] = dk.astype(BF16)
        ret_send[i, 1] = dv.astype(BF16)
        slot = 2 * chips - 2 + core
        start(before[chips], remote(ret_send.at[i], ret_recv.at[slot], r_ssem.at[i], r_rsem.at[slot], at(-chips, j)))

    send_m = remote(own_part.at[1 - core], mate_part, m_ssem.at[0], m_rsem.at[0], mate_dev)
    for j in (0, 1):
        wait_block(2 + j)
        if j == 0:
            pass_on(0)
        scores(0, (2 + j,))
        scores(1, (2 + j,))
        give_back(j, j, 1, *kv_grads(0, 2 + j, 1))

    wait_block(1)
    scores(0, (1,))
    scores(1, (1,))
    give_back(3, 1, 2, *kv_grads(0, 1, 1))
    wait_block(0)
    scores(0, (0,))
    r0 = pl.ds(0, half)
    c0 = pl.ds(0, TOK)
    give_back(2, 0, 2, dot(qt[:, r0], d_buf[r0, c0], NN), dot(gt[:, r0], p_buf[r0, c0], NN))

    def query_grads(qb, i):
        keys = kvs[pl.ds(qb, 5), 0].reshape(5 * TOK, HD)
        r = pl.ds(pl.multiple_of(qb * half + i * (half // PIECES), half // PIECES), half // PIECES)
        c = pl.ds(pl.multiple_of(qb * TOK, TOK), 5 * TOK)
        return (dot(d_buf[r, c], keys, NN) * SCALE).reshape(GROUP // PIECES, TOK, HD)

    sends_dq = []
    for i in range(PIECES):
        dq_send[i] = query_grads(1 - core, i)
        c = remote(dq_send.at[i], dq_recv.at[i], dq_ssem.at[i], dq_rsem.at[i], mate_dev)
        c.start()
        sends_dq.append(c)
    own_grads(1)
    send_m.start()

    def put(group, x):
        dq_ref[:, pl.ds(pl.multiple_of(GROUP * group, GROUP), GROUP)] = jnp.swapaxes(x, 0, 1)

    put(core, jnp.concatenate([query_grads(core, i) for i in range(PIECES)], axis=0))
    for c in sends_dq:
        c.wait_recv()
    put(1 - core, dq_recv[...].reshape(GROUP, TOK, HD))

    send_m.wait_recv()
    for i in range(4):
        wait_return(i)

    def add_up(part, h):
        x = part + ret_recv[h].astype(F32) + ret_recv[2 + h].astype(F32)
        totals[0, h] = x[0].T * SCALE
        totals[1, h] = x[1].T

    add_up(own_part[core], core)
    add_up(mate_part[...], 1 - core)
    dkv_ref[0] = jnp.swapaxes(totals[0], 0, 1)
    dkv_ref[1] = jnp.swapaxes(totals[1], 0, 1)
    for s in [send_kv, send_g, send_q, send_a, send_m] + sends_dq:
        s.wait_send()
    for there, copy in started:
        pl.when(there)(copy.wait_send)


def write_out(dq_in, dkv_in, dq_ref, dk_ref, dv_ref, sems):
    copies = [pltpu.make_async_copy(src, dst, sems.at[i])
              for i, (src, dst) in enumerate(((dq_in, dq_ref), (dkv_in.at[0], dk_ref), (dkv_in.at[1], dv_ref)))]
    for c in copies:
        c.start()
    for c in copies:
        c.wait()


def shards(n_ctx, queries, keys, values, attn_out, grad_out, log_norm, doc_lengths, doc_weight):
    any_space = pl.BlockSpec(memory_space=pl.ANY)
    smem = pl.BlockSpec(memory_space=pltpu.SMEM)
    vmem = pl.BlockSpec(memory_space=pltpu.VMEM)
    dma = pltpu.SemaphoreType.DMA
    q_shape, k_shape = queries.shape, keys.shape
    wide = 2 * GROUP * TOK

    def buf(*shape, dtype=BF16):
        return pltpu.VMEM(shape, dtype)

    dq, dkv = pl.pallas_call(
        functools.partial(kernel, n_ctx),
        out_shape=(
            buf(*q_shape, dtype=F32),
            buf(2, *k_shape, dtype=F32),
        ),
        in_specs=[any_space] * 6 + [smem] * 2,
        out_specs=(vmem, vmem),
        scratch_shapes=[
            buf(*q_shape), buf(*k_shape), buf(*k_shape), buf(*q_shape), buf(*q_shape), buf(2 * GROUP, TOK, dtype=F32),
            buf(2, 2, TOK, HD), buf(6, 2, TOK, HD), buf(6, TOK, HD),
            buf(2 * GROUP, TOK, HD), buf(2 * GROUP, TOK, HD), buf(TOK, HD),
            buf(2, GROUP, TOK, HD), buf(2, GROUP, TOK, HD), buf(2, TOK, HD),
            buf(2, GROUP, TOK, HD), buf(2, GROUP, TOK, HD),
            buf(HD, wide), buf(HD, wide),
            buf(wide, 6 * TOK), buf(wide, 6 * TOK),
            buf(2, 2, HD, TOK, dtype=F32), buf(2, HD, TOK, dtype=F32),
            buf(4, 2, HD, TOK), buf(4, 2, HD, TOK),
            buf(PIECES, GROUP // PIECES, TOK, HD, dtype=F32), buf(PIECES, GROUP // PIECES, TOK, HD, dtype=F32),
            buf(2, 2, TOK, HD, dtype=F32),
            dma((6,)), dma((5,)), dma((6,)), dma((3,)), dma((3,)), dma((4,)), dma((4,)), dma((1,)), dma((1,)),
            dma((PIECES,)), dma((PIECES,)), buf(2, TOK, HD), dma((2,)), dma((1,)),
        ],
        compiler_params=pltpu.CompilerParams(collective_id=0, has_side_effects=True, vmem_limit_bytes=52 << 20),
    )(queries, keys, values, attn_out, grad_out, log_norm, doc_lengths, doc_weight)
    dq = pltpu.with_memory_space_constraint(dq, pltpu.VMEM)
    dkv = pltpu.with_memory_space_constraint(dkv, pltpu.VMEM)
    return pl.pallas_call(
        write_out,
        out_shape=tuple(jax.ShapeDtypeStruct(shape, F32) for shape in (q_shape, k_shape, k_shape)),
        in_specs=[vmem] * 2,
        out_specs=(any_space,) * 3,
        scratch_shapes=[dma((3,))],
        compiler_params=pltpu.CompilerParams(vmem_limit_bytes=16 << 20),
    )(dq, dkv)


def solution(mesh):
    return jax.shard_map(
        functools.partial(shards, mesh.shape["ctx"]),
        mesh=mesh,
        in_specs=(
            P("ctx", "tp", None),
            P("ctx", "tp", None),
            P("ctx", "tp", None),
            P("ctx", "tp", None),
            P("ctx", "tp", None),
            P("tp", "ctx"),
            P(),
            P(),
        ),
        out_specs=(P("ctx", "tp", None), P("ctx", "tp", None), P("ctx", "tp", None)),
        check_vma=False,
    )
```

```python
import functools

import jax
import jax.numpy as jnp
from jax import lax
from jax.experimental import pallas as pl
from jax.experimental.pallas import tpu as pltpu
from jax.sharding import PartitionSpec as P

MESH = pl.DeviceIdType.MESH
F32, BF16 = jnp.float32, jnp.bfloat16
NT = (((1,), (1,)), ((), ()))
NN = (((1,), (0,)), ((), ()))

TOK = 256
HD = 128
GROUP = 8
DOCS = 32
RING = 4
PIECES = 2
SCALE = HD ** -0.5
DOC_LANE = 64
FAR_AWAY = 16384.0


def dot(a, b, dims):
    return lax.dot_general(a, b, dims, preferred_element_type=F32)


def iota(shape, dim):
    return lax.broadcasted_iota(jnp.int32, shape, dim)


def kernel(n_ctx, q_hbm, k_hbm, v_hbm, o_hbm, g_hbm, ln_hbm, dl_ref, dw_ref, dq_ref, dkv_ref,
           q_in, k_in, v_in, o_in, g_in, ln_in,
           kv_send, kvs, kaug, q_all, g_all, a_all, q_s, g_s, a_s, xaug, yaug, qt, gt,
           p_buf, d_buf, own_part, mate_part, ret_send, ret_recv, dq_send, dq_recv, totals,
           in_sem, kv_ssem, kv_rsem, x_ssem, x_rsem, r_ssem, r_rsem, m_ssem, m_rsem, dq_ssem, dq_rsem, hop, hop_ssem, hop_rsem):
    me = lax.axis_index("ctx")
    tp = lax.axis_index("tp")
    core = lax.rem(me, 2)
    chip2 = me - core
    mate = chip2 + 1 - core
    before = {1: chip2 >= 2, 2: chip2 >= 4}
    after = {1: chip2 < n_ctx - 2, 2: chip2 < n_ctx - 4}

    chip = chip2 // 2
    base, y = chip // RING * RING, lax.rem(chip, RING)
    down, up = base + lax.rem(y + RING - 1, RING), base + lax.rem(y + 1, RING)
    origin = lax.rem(chip + n_ctx // 2 - 2, n_ctx // 2)
    relay = origin // RING * RING + lax.rem(origin + RING - 1, RING)
    hop_from_here = after[2] & (core == 1)
    hop_through_here = up + 2 < n_ctx // 2
    hop_end = lax.rem(up + 2, n_ctx // 2)

    def at(chips, j):
        return (lax.rem(chip2 + 2 * chips + j + n_ctx, n_ctx), tp)

    def remote(src, dst, ssem, rsem, dev):
        return pltpu.make_async_remote_copy(src_ref=src, dst_ref=dst, send_sem=ssem, recv_sem=rsem,
                                            device_id=dev, device_id_type=MESH)

    mate_dev = (mate, tp)
    loads = [pltpu.make_async_copy(s, d, in_sem.at[i]) for i, (s, d) in enumerate(
        [(k_hbm, k_in), (v_hbm, v_in), (g_hbm, g_in), (o_hbm, o_in), (q_hbm, q_in), (ln_hbm, ln_in)])]
    loads[0].start()
    loads[1].start()
    barrier = pltpu.get_barrier_semaphore()
    pl.semaphore_signal(barrier, inc=1, device_id=mate_dev, device_id_type=MESH)
    greeted = 1
    for chips, there in ((1, after[1]), (2, after[2]), (-1, before[1]), (-2, before[2])):
        greeted = greeted + 2 * there.astype(jnp.int32)

        @pl.when(there)
        def _():
            for j in (0, 1):
                pl.semaphore_signal(barrier, inc=1, device_id=at(chips, j), device_id_type=MESH)

    for there, devs in ((hop_from_here, [(2 * down, tp), (2 * down + 1, tp)]),
                        (hop_through_here, [(2 * up + 1, tp), (2 * hop_end + core, tp)]),
                        (before[2], [(2 * relay + core, tp)])):
        greeted = greeted + len(devs) * there.astype(jnp.int32)

        @pl.when(there)
        def _():
            for dev in devs:
                pl.semaphore_signal(barrier, inc=1, device_id=dev, device_id_type=MESH)

    for load in loads[2:]:
        load.start()
    loads[0].wait()
    kv_send[:, 0] = jnp.swapaxes(k_in[...], 0, 1)
    loads[1].wait()
    kv_send[:, 1] = jnp.swapaxes(v_in[...], 0, 1)
    kvs[4 + core] = kv_send[core]

    lane1 = iota((1, HD), 1)
    starts = jnp.full((1, HD), 1 << 30, jnp.int32)
    ends = jnp.zeros((1, HD), jnp.int32)
    weights = jnp.zeros((1, HD), F32)
    run = jnp.int32(0)
    total = jnp.int32(0)
    for d in range(DOCS):
        here = lane1 == DOC_LANE + d
        length = dl_ref[d]
        weight = dw_ref[d]
        starts = jnp.where(here, run, starts)
        run = run + length
        ends = jnp.where(here, run, ends)
        weights = jnp.where(here, weight.astype(F32), weights)
        total = total + length * weight

    rows = iota((TOK, HD), 0)
    lanes = iota((TOK, HD), 1)

    def one_hot(block):
        pos = block * TOK + rows
        return (pos >= starts) & (pos < ends)

    for kb in range(6):
        hot = one_hot(chip2 - 4 + kb)
        extra = jnp.where(lanes < 48, 1.0, jnp.where((lanes >= DOC_LANE) & (lanes < DOC_LANE + DOCS) & ~hot, -FAR_AWAY, 0.0))
        kaug[kb] = extra.astype(BF16)

    scale = jnp.sum(jnp.where(one_hot(me), weights, 0.0), axis=1, keepdims=True)
    scale = scale * float(n_ctx * TOK) / total.astype(F32)
    scale = jnp.broadcast_to(scale, (TOK, HD))

    loads[2].wait()
    g_all[...] = jnp.swapaxes(g_in[...], 0, 1)
    loads[3].wait()
    q_all[...] = jnp.swapaxes(o_in[...], 0, 1)
    lane_slot = jnp.where(lane1 >= DOC_LANE, lax.rem(lane1, 16), -1)
    delta = jnp.zeros((TOK, HD), F32)
    for h in range(2 * GROUP):
        g = g_all[h].astype(F32)
        summed = jnp.sum(g * q_all[h].astype(F32), axis=1, keepdims=True)
        delta = jnp.where(lane_slot == h, summed, delta)
        g_all[h] = (g * scale).astype(BF16)

    pl.semaphore_wait(barrier, greeted)

    started = []

    def start(there, copy):
        @pl.when(there)
        def _():
            copy.start()
        started.append((there, copy))

    send_kv = remote(kv_send.at[1 - core], kvs.at[4 + core], kv_ssem.at[0], kv_rsem.at[4 + core], mate_dev)
    send_kv.start()

    def send_near(j):
        for h in (0, 1):
            start(after[1] & (core == j),
                  remote(kv_send.at[h], kvs.at[2 + core], kv_ssem.at[1 + h], kv_rsem.at[2 + core], at(1, h)))

    send_near(0)

    def arrive(there, landed, copy):
        @pl.when(there)
        def _():
            copy.wait_recv()

        @pl.when(jnp.logical_not(there))
        def _():
            landed[...] = jnp.zeros(landed.shape, landed.dtype)

    def wait_block(kb):
        arrive(before[2 - kb // 2], kvs.at[kb],
               remote(kv_send.at[0], kvs.at[kb], kv_ssem.at[0], kv_rsem.at[kb], mate_dev))

    def wait_return(i):
        arrive(after[1 + i // 2], ret_recv.at[i],
               remote(ret_send.at[0], ret_recv.at[i], r_ssem.at[0], r_rsem.at[i], mate_dev))

    def wait_mate():
        remote(kv_send.at[0], kvs.at[5 - core], kv_ssem.at[0], kv_rsem.at[5 - core], mate_dev).wait_recv()

    for h in (0, 1):
        start(hop_from_here, remote(kv_send.at[h], hop, hop_ssem.at[h], hop_rsem.at[0], (2 * down + h, tp)))

    send_g = remote(g_all.at[pl.ds(GROUP * (1 - core), GROUP)], g_s.at[core], x_ssem.at[0], x_rsem.at[0], mate_dev)
    send_g.start()
    loads[4].wait()
    q_all[...] = jnp.swapaxes(q_in[...], 0, 1)
    send_q = remote(q_all.at[pl.ds(GROUP * (1 - core), GROUP)], q_s.at[core], x_ssem.at[1], x_rsem.at[1], mate_dev)
    send_q.start()
    g_s[core] = g_all[pl.ds(GROUP * core, GROUP)]
    q_s[core] = q_all[pl.ds(GROUP * core, GROUP)]

    loads[5].wait()
    ln = ln_in[...]
    norm = jnp.concatenate([ln, ln, ln, jnp.zeros((80, TOK), F32)], axis=0).T
    z = jnp.where(lanes < 48, norm * (-(HD ** 0.5)), -(delta * scale))
    hi = z.astype(BF16)
    rest = z - hi.astype(F32)
    mid = rest.astype(BF16)
    low = (rest - mid.astype(F32)).astype(BF16)
    term = lax.rem(lanes, 64) // 16
    a_all[...] = jnp.where(term == 0, hi.astype(F32), jnp.where(term == 1, mid.astype(F32), low.astype(F32))).astype(BF16)
    send_a = remote(a_all, a_s.at[core], x_ssem.at[2], x_rsem.at[2], mate_dev)
    send_a.start()
    a_s[core] = a_all[...]

    def prepare(qb):
        a = a_s[qb].astype(F32)
        hot = one_hot(chip2 + qb)
        base = jnp.where(hot, 1.0, 0.0)
        slot = lax.rem(lanes, 16)
        for g in range(GROUP):
            mine = slot == GROUP * core + g
            xaug[qb, g] = jnp.where(mine & (lanes < 48), a, base).astype(BF16)
            yaug[qb, g] = jnp.where(mine & (lanes >= 64) & (lanes < 112), a, 0.0).astype(BF16)
            cols = pl.ds(pl.multiple_of((qb * GROUP + g) * TOK, TOK), TOK)
            qt[:, cols] = q_s[qb, g].T
            gt[:, cols] = g_s[qb, g].T

    ones = jnp.ones((TOK, HD), BF16)

    def keys_of(kbs):
        return jnp.concatenate([jnp.concatenate([kvs[kb, 0], kaug[kb]], axis=1) for kb in kbs], axis=0)

    def values_of(kbs):
        return jnp.concatenate([jnp.concatenate([kvs[kb, 1], ones], axis=1) for kb in kbs], axis=0)

    causal = iota((TOK, TOK), 0) >= iota((TOK, TOK), 1)

    def scores(qb, kbs, diagonal=False):
        width = TOK * len(kbs)
        cols = pl.ds(pl.multiple_of(kbs[0] * TOK, TOK), width)
        keys, values = keys_of(kbs), values_of(kbs)
        for g in range(GROUP):
            x = jnp.concatenate([q_s[qb, g], xaug[qb, g]], axis=1)
            y = jnp.concatenate([g_s[qb, g], yaug[qb, g]], axis=1)
            p = jnp.exp(dot(x, keys, NT) * SCALE)
            if diagonal:
                p = jnp.where(causal, p, 0.0)
            ds = p * dot(y, values, NT)
            at_rows = pl.ds(pl.multiple_of((qb * GROUP + g) * TOK, TOK), TOK)
            p_buf[at_rows, cols] = p.astype(BF16)
            d_buf[at_rows, cols] = ds.astype(BF16)

    half = GROUP * TOK

    def kv_grads(first_row, kb, count):
        r = pl.ds(first_row, 2 * half - first_row) if first_row else slice(None)
        c = pl.ds(kb * TOK, count * TOK)
        return dot(qt[:, r], d_buf[r, c], NN), dot(gt[:, r], p_buf[r, c], NN)

    prepare(core)
    scores(core, (4 + core,), True)
    wait_mate()
    for s in (send_g, send_q, send_a):
        s.wait_recv()
    prepare(1 - core)
    send_near(1)

    scores(1 - core, (5 - core,), True)
    scores(1, (4,))

    @pl.when(hop_through_here)
    def _():
        remote(kv_send.at[0], hop, hop_ssem.at[0], hop_rsem.at[0], mate_dev).wait_recv()
    start(hop_through_here, remote(hop, kvs.at[1], kv_ssem.at[4], kv_rsem.at[1], (2 * hop_end + core, tp)))

    def own_grads(j):
        dk, dv = kv_grads(j * half, 4 + j, 1)
        own_part[j, 0] = dk
        own_part[j, 1] = dv

    def pass_on(j):
        start(before[1] & after[1],
              remote(kvs.at[2 + j], kvs.at[j], kv_ssem.at[3 + j], kv_rsem.at[j], at(1, core)))

    wait_block(2)
    pass_on(0)
    own_grads(0)

    def give_back(i, j, chips, dk, dv):
        ret_send[i, 0] = dk.astype(BF16)
        ret_send[i, 1] = dv.astype(BF16)
        slot = 2 * chips - 2 + core
        start(before[chips], remote(ret_send.at[i], ret_recv.at[slot], r_ssem.at[i], r_rsem.at[slot], at(-chips, j)))

    send_m = remote(own_part.at[1 - core], mate_part, m_ssem.at[0], m_rsem.at[0], mate_dev)
    for j in (0, 1):
        if j == 1:
            wait_block(3)
        scores(0, (2 + j,))
        scores(1, (2 + j,))
        give_back(j, j, 1, *kv_grads(0, 2 + j, 1))

    wait_block(1)
    scores(0, (1,))
    scores(1, (1,))
    give_back(3, 1, 2, *kv_grads(0, 1, 1))
    wait_block(0)
    scores(0, (0,))
    r0 = pl.ds(0, half)
    c0 = pl.ds(0, TOK)
    give_back(2, 0, 2, dot(qt[:, r0], d_buf[r0, c0], NN), dot(gt[:, r0], p_buf[r0, c0], NN))

    def query_grads(qb, i):
        keys = kvs[pl.ds(qb, 5), 0].reshape(5 * TOK, HD)
        r = pl.ds(pl.multiple_of(qb * half + i * (half // PIECES), half // PIECES), half // PIECES)
        c = pl.ds(pl.multiple_of(qb * TOK, TOK), 5 * TOK)
        return (dot(d_buf[r, c], keys, NN) * SCALE).reshape(GROUP // PIECES, TOK, HD)

    sends_dq = []
    for i in range(PIECES):
        dq_send[i] = query_grads(1 - core, i)
        c = remote(dq_send.at[i], dq_recv.at[i], dq_ssem.at[i], dq_rsem.at[i], mate_dev)
        c.start()
        sends_dq.append(c)
    own_grads(1)
    send_m.start()

    def put(group, x):
        dq_ref[:, pl.ds(pl.multiple_of(GROUP * group, GROUP), GROUP)] = jnp.swapaxes(x, 0, 1)

    put(core, jnp.concatenate([query_grads(core, i) for i in range(PIECES)], axis=0))
    for c in sends_dq:
        c.wait_recv()
    put(1 - core, dq_recv[...].reshape(GROUP, TOK, HD))

    send_m.wait_recv()
    for i in range(4):
        wait_return(i)

    def add_up(part, h):
        x = part + ret_recv[h].astype(F32) + ret_recv[2 + h].astype(F32)
        totals[0, h] = x[0].T * SCALE
        totals[1, h] = x[1].T

    add_up(own_part[core], core)
    add_up(mate_part[...], 1 - core)
    dkv_ref[0] = jnp.swapaxes(totals[0], 0, 1)
    dkv_ref[1] = jnp.swapaxes(totals[1], 0, 1)
    for s in [send_kv, send_g, send_q, send_a, send_m] + sends_dq:
        s.wait_send()
    for there, copy in started:
        pl.when(there)(copy.wait_send)


def write_out(dq_in, dkv_in, dq_ref, dk_ref, dv_ref, sems):
    copies = [pltpu.make_async_copy(src, dst, sems.at[i])
              for i, (src, dst) in enumerate(((dq_in, dq_ref), (dkv_in.at[0], dk_ref), (dkv_in.at[1], dv_ref)))]
    for c in copies:
        c.start()
    for c in copies:
        c.wait()


def shards(n_ctx, queries, keys, values, attn_out, grad_out, log_norm, doc_lengths, doc_weight):
    any_space = pl.BlockSpec(memory_space=pl.ANY)
    smem = pl.BlockSpec(memory_space=pltpu.SMEM)
    vmem = pl.BlockSpec(memory_space=pltpu.VMEM)
    dma = pltpu.SemaphoreType.DMA
    q_shape, k_shape = queries.shape, keys.shape
    wide = 2 * GROUP * TOK

    def buf(*shape, dtype=BF16):
        return pltpu.VMEM(shape, dtype)

    dq, dkv = pl.pallas_call(
        functools.partial(kernel, n_ctx),
        out_shape=(
            buf(*q_shape, dtype=F32),
            buf(2, *k_shape, dtype=F32),
        ),
        in_specs=[any_space] * 6 + [smem] * 2,
        out_specs=(vmem, vmem),
        scratch_shapes=[
            buf(*q_shape), buf(*k_shape), buf(*k_shape), buf(*q_shape), buf(*q_shape), buf(2 * GROUP, TOK, dtype=F32),
            buf(2, 2, TOK, HD), buf(6, 2, TOK, HD), buf(6, TOK, HD),
            buf(2 * GROUP, TOK, HD), buf(2 * GROUP, TOK, HD), buf(TOK, HD),
            buf(2, GROUP, TOK, HD), buf(2, GROUP, TOK, HD), buf(2, TOK, HD),
            buf(2, GROUP, TOK, HD), buf(2, GROUP, TOK, HD),
            buf(HD, wide), buf(HD, wide),
            buf(wide, 6 * TOK), buf(wide, 6 * TOK),
            buf(2, 2, HD, TOK, dtype=F32), buf(2, HD, TOK, dtype=F32),
            buf(4, 2, HD, TOK), buf(4, 2, HD, TOK),
            buf(PIECES, GROUP // PIECES, TOK, HD, dtype=F32), buf(PIECES, GROUP // PIECES, TOK, HD, dtype=F32),
            buf(2, 2, TOK, HD, dtype=F32),
            dma((6,)), dma((5,)), dma((6,)), dma((3,)), dma((3,)), dma((4,)), dma((4,)), dma((1,)), dma((1,)),
            dma((PIECES,)), dma((PIECES,)), buf(2, TOK, HD), dma((2,)), dma((1,)),
        ],
        compiler_params=pltpu.CompilerParams(collective_id=0, has_side_effects=True, vmem_limit_bytes=52 << 20),
    )(queries, keys, values, attn_out, grad_out, log_norm, doc_lengths, doc_weight)
    dq = pltpu.with_memory_space_constraint(dq, pltpu.VMEM)
    dkv = pltpu.with_memory_space_constraint(dkv, pltpu.VMEM)
    return pl.pallas_call(
        write_out,
        out_shape=tuple(jax.ShapeDtypeStruct(shape, F32) for shape in (q_shape, k_shape, k_shape)),
        in_specs=[vmem] * 2,
        out_specs=(any_space,) * 3,
        scratch_shapes=[dma((3,))],
        compiler_params=pltpu.CompilerParams(vmem_limit_bytes=16 << 20),
    )(dq, dkv)


def solution(mesh):
    return jax.shard_map(
        functools.partial(shards, mesh.shape["ctx"]),
        mesh=mesh,
        in_specs=(
            P("ctx", "tp", None),
            P("ctx", "tp", None),
            P("ctx", "tp", None),
            P("ctx", "tp", None),
            P("ctx", "tp", None),
            P("tp", "ctx"),
            P(),
            P(),
        ),
        out_specs=(P("ctx", "tp", None), P("ctx", "tp", None), P("ctx", "tp", None)),
        check_vma=False,
    )
```
